32 devices in a mesh: row: 8 (over z, y), col: 4 (over x, core).
Axes of the slice: x: 2, y: 2, z: 4, core: 2. Of those that a mesh axis runs over, the one named last changes fastest.
Arguments:
- features: bfloat16 [8192, 256], P(('row', 'col')), may hold values from -6 to 6
- weight: bfloat16 [256, 256], replicated, may hold values from -0.375 to 0.375
- bias: float32 [256], replicated, may hold values from -3 to 3
- block_values: bfloat16 [8, 4, 32, 128, 128], P('row', 'col'), may hold values from -0.1875 to 0.1875
- block_target: int32 [8, 4, 32], P('row', 'col'), may hold values from 0 to 9
- block_source: int32 [8, 4, 32], P('row', 'col'), may hold values from 0 to 7
- block_count: int32 [8, 4], P('row', 'col'), may hold values from 4 to 32, as said below
- cotangent: bfloat16 [8192, 256], P(('row', 'col')), may hold values from -6 to 6
Outputs:
- output: bfloat16 [8192, 256], P(('row', 'col'))
- grad_inputs: bfloat16 [8192, 256], P(('row', 'col'))
- grad_weight: float32 [256, 256], replicated
- grad_bias: float32 [256], replicated
The draws below stay inside these ranges and needn't reach their ends.
Inputs may be any that keep to these rules, and one draw needn't show every extreme that they name: `block_count`: slots at or after a device's count hold no adjacency block; some device uses all 32 slots.
All inputs are finite; a program needn't handle non-finite values.
Results may differ from the reference program's by a relative error of at most 0.006.
Values may be sent and summed in bfloat16 or wider, within the bound.
No kernel may reach another device: no remote copies, remote signals or barrier semaphores. Data moves between devices by JAX's collectives and lax.ppermute only.
A program may use at most 64 MiB of HBM per device.

```python
import math
import jax
import jax.numpy as jnp
from jax import lax

BLK = 128
F = 256
HALF = 2
VB = 2
NB = 32
DB = 10
SB = 8
NODES = 8192
N_ROW = 8
N_COL = 4


def draw_block_count(key, part):
    key_counts, key_choice = jax.random.split(key)
    counts_drawn = jax.random.randint(key_counts, (N_ROW, N_COL), max(NB // 8, 1), 3 * NB // 4 + 1, dtype=jnp.int32)
    chosen_device = jax.random.randint(key_choice, (), 0, N_ROW * N_COL, dtype=jnp.int32)
    flat_counts = counts_drawn.reshape(-1)
    device_ids = jnp.arange(N_ROW * N_COL, dtype=jnp.int32)
    flat_counts = jnp.where(device_ids == chosen_device, jnp.int32(NB), flat_counts)
    return flat_counts.reshape(N_ROW, N_COL).astype(jnp.int32)


def place_ends(result, stream_key, least, top_value):
    extent = result.shape
    index_at = [jax.random.randint(jax.random.fold_in(stream_key, axis), (), 0, extent[axis]) for axis in range(len(extent))]
    result = result.at[tuple(index_at)].set(least)
    longest = extent.index(max(extent))
    index_at[longest] = (index_at[longest] + 1) % extent[longest]
    return result.at[tuple(index_at)].set(top_value)


def shard_levels(key, shape, shards, least, high):
    factor_of = 1.0
    for dim, parts in shards:
        steps = jax.random.uniform(jax.random.fold_in(jax.random.fold_in(key, 6), dim), (parts,), jnp.float32, least / len(shards), high / len(shards))
        factor_of = factor_of * jnp.repeat(jnp.exp(steps), shape[dim] // parts).reshape((-1,) + (1,) * (len(shape) - 1 - dim))
    return factor_of


def normal_values(key, dims, width, most, cuts=(), held_as=jnp.bfloat16):
    factor_of = shard_levels(key, dims, cuts, -0.22, 0.18) if cuts else 1.0
    values = jax.random.normal(key, dims, jnp.float32) * width * factor_of
    return jnp.minimum(jnp.maximum(values, -most), most).astype(held_as)


def setup_inputs(seed: int = 0) -> dict:
    key_list = jax.random.split(jax.random.key(seed), 9)
    return {
        "features": normal_values(key_list[0], (NODES, F), 1.0, 6.0, ((0, 32),)),
        "weight": normal_values(key_list[1], (F, F), F ** -0.5, 0.375),
        "bias": normal_values(key_list[2], (F,), 0.5, 3.0, (), jnp.float32),
        "block_values": normal_values(key_list[3], (N_ROW, N_COL, NB, BLK, BLK), 1024 ** -0.5, 0.1875, ((0, 8), (1, 4))),
        "block_target": place_ends(jax.random.randint(key_list[4], (N_ROW, N_COL, NB), 0, DB), jax.random.fold_in(key_list[4], 1), 0, DB - 1).astype(jnp.int32),
        "block_source": place_ends(jax.random.randint(key_list[5], (N_ROW, N_COL, NB), 0, SB), jax.random.fold_in(key_list[5], 1), 0, SB - 1).astype(jnp.int32),
        "block_count": draw_block_count(jax.random.fold_in(key_list[8], 71), 0),
        "cotangent": normal_values(key_list[7], (NODES, F), 1.0, 6.0, ((0, 32),)),
    }


def silu_slope(argument):
    sigmoid_value = jax.nn.sigmoid(argument)
    return sigmoid_value * (1.0 + argument * (1.0 - sigmoid_value))

def reference(features, weight, bias, block_values, block_target, block_source, block_count, cotangent):
    span_count = 2 * HALF + 1
    dest_total = span_count * VB
    source_total = N_COL * VB
    hidden = jnp.dot(features, weight, preferred_element_type=jnp.float32).astype(jnp.bfloat16)
    hidden_blocks = hidden.reshape(N_ROW, source_total, BLK, F)
    slot_ids = jnp.arange(NB, dtype=jnp.int32)
    live_all = (slot_ids[None, None, :] < block_count[:, :, None]).astype(jnp.float32)
    dest_ids = jnp.arange(dest_total, dtype=jnp.int32)
    source_ids = jnp.arange(source_total, dtype=jnp.int32)
    row_ids = jnp.arange(N_ROW, dtype=jnp.int32)

    def forward_row(accumulated, row_index):
        row_sources = hidden_blocks[row_index]
        picked = jnp.take(row_sources, block_source[row_index], axis=0)
        products = jnp.einsum('csij,csjf->csif', block_values[row_index].astype(jnp.float32), picked.astype(jnp.float32), precision=lax.Precision.HIGHEST)
        selector = (block_target[row_index][:, None, :] == dest_ids[None, :, None]).astype(jnp.float32) * live_all[row_index][:, None, :]
        partial_value = jnp.einsum('cds,csif->cdif', selector, products, precision=lax.Precision.HIGHEST)
        partial_value = partial_value.reshape(N_COL, span_count, VB, BLK, F)
        for offset in range(span_count):
            target_row = ((row_index + offset - HALF) % N_ROW).astype(jnp.int32)
            accumulated = accumulated.at[target_row].add(partial_value[:, offset])
        return (accumulated, None)
    start_sum = jnp.zeros((N_ROW, N_COL, VB, BLK, F), jnp.float32)
    aggregate, _ = lax.scan(forward_row, start_sum, row_ids)
    aggregate = aggregate.reshape(NODES, F)
    pre_value = aggregate + bias.astype(jnp.float32)[None, :]
    output = jax.nn.silu(pre_value).astype(jnp.bfloat16)
    grad_pre_exact = cotangent.astype(jnp.float32) * silu_slope(pre_value)
    grad_pre = grad_pre_exact.astype(jnp.bfloat16)
    grad_blocks = grad_pre.reshape(N_ROW, N_COL, VB, BLK, F)

    def backward_row(unused, row_index):
        fetched = jnp.stack([grad_blocks[((row_index + offset - HALF) % N_ROW).astype(jnp.int32)] for offset in range(span_count)], axis=1)
        fetched = fetched.reshape(N_COL, dest_total, BLK, F)
        picked = jax.vmap(lambda table_rows, chosen: jnp.take(table_rows, chosen, axis=0))(fetched, block_target[row_index])
        products = jnp.einsum('csji,csjf->csif', block_values[row_index].astype(jnp.float32), picked.astype(jnp.float32), precision=lax.Precision.HIGHEST)
        selector = (block_source[row_index][:, None, :] == source_ids[None, :, None]).astype(jnp.float32) * live_all[row_index][:, None, :]
        sums = jnp.einsum('cbs,csif->bif', selector, products, precision=lax.Precision.HIGHEST)
        return (unused, sums)
    _, source_sums = lax.scan(backward_row, jnp.zeros((), jnp.float32), row_ids)
    grad_source = source_sums.reshape(NODES, F).astype(jnp.bfloat16)
    grad_inputs = lax.dot_general(grad_source, weight, (((1,), (1,)), ((), ())), preferred_element_type=jnp.float32).astype(jnp.bfloat16)
    normalizer = 1.0 / math.sqrt(NODES)
    grad_weight = jnp.dot(features.T, grad_source, preferred_element_type=jnp.float32) * normalizer
    grad_bias = lax.optimization_barrier(jnp.sum(grad_pre_exact, axis=0)) * normalizer
    return (output, grad_inputs, grad_weight, grad_bias)
```

```python
import functools
import math

import jax
import jax.numpy as jnp
from jax import lax
from jax.experimental import pallas as pl
from jax.experimental.pallas import tpu as pltpu
from jax.sharding import PartitionSpec as P

BLK = 128
HALF = 2
VB = 2
SPAN = 2 * HALF + 1
SLICE = 8
SLOT_GROUP = 8
VMEM = pltpu.VMEM
SMEM = pltpu.SMEM


def shifted(block, axis, distance):
    size = lax.axis_size(axis)
    return lax.ppermute(block, axis, [(i, (i + distance) % size) for i in range(size)])


def swapped(block, axis, bit):
    size = lax.axis_size(axis)
    return lax.ppermute(block, axis, [(i, i ^ bit) for i in range(size)])


def spec(space):
    return pl.BlockSpec(memory_space=space)


def call(body, outs, scratch, flops, spaces, name):
    return pl.pallas_call(
        body,
        out_shape=outs,
        in_specs=[spec(space) for space in spaces],
        out_specs=[spec(VMEM)] * len(outs),
        scratch_shapes=scratch,
        name=name,
        cost_estimate=pl.CostEstimate(flops=flops, bytes_accessed=2**20, transcendentals=0),
        compiler_params=pltpu.CompilerParams(vmem_limit_bytes=16 * 2**20),
    )


def for_slots(slot_total, live, step):
    for start in range(0, slot_total, SLOT_GROUP):

        @pl.when(start < live)
        def _group():
            for slot in range(start, min(start + SLOT_GROUP, slot_total)):
                step(slot)


def forward_kernel(
    count, target, source, values, own, near, across, far,
    mine, down2, down1, up1, up2, table, totals,
):
    column = lax.axis_index("col")
    live = count[0, 0]
    for relative, part in enumerate((own, near, across, far)):
        for block in range(VB):
            table[relative * VB + block] = part[block * BLK : (block + 1) * BLK, :]
    totals[...] = jnp.zeros_like(totals)

    def step(slot):
        block = source[0, 0, slot]
        place = ((block // VB) ^ column) * VB + lax.rem(block, VB)
        goal = jnp.where(slot < live, target[0, 0, slot], SPAN * VB)
        totals[goal] += jnp.dot(
            values[0, 0, slot], table[place], preferred_element_type=jnp.float32
        )

    for_slots(values.shape[2], live, step)
    for offset, out in enumerate((down2, down1, mine, up1, up2)):
        for block in range(VB):
            out[block * BLK : (block + 1) * BLK, :] = totals[offset * VB + block].astype(out.dtype)


def middle_kernel(
    mine, from_up2, from_up1, from_down1, from_down2, weight, bias, cotangent,
    output, grad_out, message,
):
    total = mine[...]
    for part in (from_up2, from_up1, from_down1, from_down2):
        total = total + part[...].astype(jnp.float32)
    high = total.astype(jnp.bfloat16)
    low = (total - high.astype(jnp.float32)).astype(jnp.bfloat16)
    kernel = weight[...]
    pre = jnp.dot(high, kernel, preferred_element_type=jnp.float32)
    pre = pre + jnp.dot(low, kernel, preferred_element_type=jnp.float32) + bias[...]
    gate = 1.0 / (1.0 + jnp.exp(-pre))
    output[...] = (pre * gate).astype(jnp.bfloat16)
    exact = cotangent[...].astype(jnp.float32) * (gate * (1.0 + pre * (1.0 - gate)))
    grad = exact.astype(jnp.bfloat16)
    grad_out[...] = lax.dot_general(
        kernel, grad, (((1,), (1,)), ((), ())), preferred_element_type=jnp.float32
    ).astype(jnp.bfloat16)
    weight_term = lax.dot_general(
        high, grad, (((0,), (0,)), ((), ())), preferred_element_type=jnp.float32
    )
    bias_term = jnp.sum(exact, axis=0, keepdims=True)
    bias_high = bias_term.astype(jnp.bfloat16).astype(jnp.float32)
    lines = lax.broadcasted_iota(jnp.int32, (SLICE, bias_term.shape[1]), 0)
    tail = jnp.where(lines == 0, bias_high, jnp.where(lines == 1, bias_term - bias_high, 0.0))
    for index in range(message.shape[0]):
        rows = weight_term[index * SLICE : (index + 1) * SLICE, :]
        message[index] = jnp.concatenate([rows, tail], axis=0).astype(jnp.bfloat16)


def backward_kernel(
    count, target, source, values, from_down2, from_down1, local, from_up1, from_up2,
    mine, near, across, far, table, totals,
):
    column = lax.axis_index("col")
    live = count[0, 0]
    for offset, part in enumerate((from_down2, from_down1, local, from_up1, from_up2)):
        for block in range(VB):
            table[offset * VB + block] = part[:, block * BLK : (block + 1) * BLK]
    totals[...] = jnp.zeros_like(totals)

    def step(slot):
        goal = jnp.where(slot < live, source[0, 0, slot], totals.shape[0] - 1)
        totals[goal] += jnp.dot(
            table[target[0, 0, slot]], values[0, 0, slot], preferred_element_type=jnp.float32
        )

    for_slots(values.shape[2], live, step)
    for relative, out in enumerate((mine, near, across, far)):
        for block in range(VB):
            out[:, block * BLK : (block + 1) * BLK] = totals[
                (column ^ relative) * VB + block
            ].astype(out.dtype)


def slice_kernel(scale, received, part, bias_out):
    total = jnp.sum(received[...].astype(jnp.float32), axis=0) * scale
    part[...] = jnp.broadcast_to(total[:SLICE].astype(jnp.bfloat16)[None], part.shape)
    bias_out[...] = total[SLICE : SLICE + 1] + total[SLICE + 1 : SLICE + 2]


def last_kernel(mine, near, across, far, grad_inputs):
    total = mine[...]
    for part in (near, across, far):
        total = total + part[...].astype(jnp.float32)
    grad_inputs[...] = total.T.astype(jnp.bfloat16)


def shards(
    features, weight, bias, block_values, block_target, block_source, block_count, cotangent
):
    columns = lax.axis_size("col")
    assert columns == 4
    rows = lax.axis_size("row")
    own_rows, width = features.shape
    slots = block_values.shape[2]
    sources = columns * VB
    bf16, f32 = jnp.bfloat16, jnp.float32

    near = swapped(features, "col", 1)
    across = swapped(features, "col", 2)
    far = swapped(across, "col", 1)
    whole = jax.ShapeDtypeStruct((own_rows, width), bf16)
    wide = jax.ShapeDtypeStruct((own_rows, width), f32)
    mine, down2, down1, up1, up2 = call(
        forward_kernel,
        [wide] + [whole] * 4,
        [
            pltpu.VMEM((sources, BLK, width), bf16),
            pltpu.VMEM((SPAN * VB + 1, BLK, width), f32),
        ],
        2 * slots * BLK * BLK * width,
        [SMEM] * 3 + [VMEM] * 5,
        "aggregate_terms",
    )(block_count, block_target, block_source, block_values, features, near, across, far)

    from_up2 = shifted(down2, "row", -2)
    from_down2 = shifted(up2, "row", 2)
    from_up1 = shifted(down1, "row", -1)
    from_down1 = shifted(up1, "row", 1)
    flipped = jax.ShapeDtypeStruct((width, own_rows), bf16)
    slices = width // SLICE
    output, grad_out, message = call(
        middle_kernel,
        [whole, flipped, jax.ShapeDtypeStruct((slices, 2 * SLICE, width), bf16)],
        [],
        2 * 4 * own_rows * width * width,
        [VMEM] * 8,
        "pointwise_and_weight",
    )(mine, from_up2, from_up1, from_down1, from_down2, weight, bias[None, :], cotangent)

    grad_up2 = shifted(grad_out, "row", -2)
    grad_down2 = shifted(grad_out, "row", 2)
    grad_up1 = shifted(grad_out, "row", -1)
    grad_down1 = shifted(grad_out, "row", 1)
    mine, near, across, far = call(
        backward_kernel,
        [jax.ShapeDtypeStruct((width, own_rows), f32)] + [flipped] * 3,
        [
            pltpu.VMEM((SPAN * VB, width, BLK), bf16),
            pltpu.VMEM((sources + 1, width, BLK), f32),
        ],
        2 * slots * BLK * BLK * width,
        [SMEM] * 3 + [VMEM] * 6,
        "source_terms",
    )(
        block_count, block_target, block_source, block_values,
        grad_down2, grad_down1, grad_out, grad_up1, grad_up2,
    )
    near = swapped(near, "col", 1)
    across = swapped(across, "col", 2)
    far = swapped(far, "col", 3)

    scale = 1.0 / math.sqrt(own_rows * rows * columns)
    everyone = ("row", "col")
    if slices == rows * columns:
        received = lax.all_to_all(message, everyone, 0, 0, tiled=True)
        part, bias_total = call(
            functools.partial(slice_kernel, scale),
            [
                jax.ShapeDtypeStruct((slices, SLICE, width), bf16),
                jax.ShapeDtypeStruct((1, width), f32),
            ],
            [],
            slices * SLICE * width,
            [VMEM],
            "weight_slice",
        )(received)
        weight_total = lax.all_to_all(part, everyone, 0, 0, tiled=True)
        weight_total = weight_total.reshape(width, width).astype(f32)
        bias_total = bias_total[0]
    else:
        summed = lax.psum(message.astype(f32), everyone) * scale
        weight_total = summed[:, :SLICE].reshape(width, width)
        bias_total = summed[0, SLICE] + summed[0, SLICE + 1]

    grad_inputs = call(
        last_kernel, [whole], [], own_rows * width * 4, [VMEM] * 4, "source_sum"
    )(mine, near, across, far)[0]
    return (output, grad_inputs, weight_total, bias_total)


def solution(mesh):
    return jax.shard_map(
        shards,
        mesh=mesh,
        in_specs=(
            P(("row", "col"), None),
            P(),
            P(),
            P("row", "col", None, None, None),
            P("row", "col", None),
            P("row", "col", None),
            P("row", "col"),
            P(("row", "col"), None),
        ),
        out_specs=(P(("row", "col"), None), P(("row", "col"), None), P(), P()),
        check_vma=False,
    )
```

```python
import functools
import math

import jax
import jax.numpy as jnp
from jax import lax
from jax.experimental import pallas as pl
from jax.experimental.pallas import tpu as pltpu
from jax.sharding import PartitionSpec as P

BLK = 128
HALF = 2
VB = 2
SPAN = 2 * HALF + 1
SLICE = 8
LANES = 128
SLOT_GROUP = 8
LONG = 10**11
VMEM = pltpu.VMEM
SMEM = pltpu.SMEM


def shifted(block, axis, distance):
    size = lax.axis_size(axis)
    return lax.ppermute(block, axis, [(i, (i + distance) % size) for i in range(size)])


def swapped(block, axis, bit):
    size = lax.axis_size(axis)
    return lax.ppermute(block, axis, [(i, i ^ bit) for i in range(size)])


def spec(space):
    return pl.BlockSpec(memory_space=space)


def call(body, outs, scratch, flops, spaces, name):
    return pl.pallas_call(
        body,
        out_shape=outs,
        in_specs=[spec(space) for space in spaces],
        out_specs=[spec(VMEM)] * len(outs),
        scratch_shapes=scratch,
        name=name,
        cost_estimate=pl.CostEstimate(flops=flops, bytes_accessed=2**20, transcendentals=0),
        compiler_params=pltpu.CompilerParams(vmem_limit_bytes=16 * 2**20),
    )


def for_slots(slot_total, live, step):
    for start in range(0, slot_total, SLOT_GROUP):

        @pl.when(start < live)
        def _group():
            for slot in range(start, min(start + SLOT_GROUP, slot_total)):
                step(slot)


def stage_kernel(values, own, bias, values_out, own_out, bias_out, values_sem, own_sem, bias_sem):
    copies = (
        pltpu.make_async_copy(values, values_out, values_sem),
        pltpu.make_async_copy(own, own_out, own_sem),
        pltpu.make_async_copy(bias, bias_out, bias_sem),
    )
    for copy in copies:
        copy.start()
    for copy in copies:
        copy.wait()


def table_kernel(own, near, across, head):
    for relative, part in enumerate((own, near, across)):
        for block in range(VB):
            head[relative * VB + block] = part[block * BLK : (block + 1) * BLK, :]


def forward_kernel(
    count, target, source, values, head, far,
    mine, down2, down1, up1, up2, table, totals,
):
    column = lax.axis_index("col")
    live = count[0, 0]
    known = head.shape[0]
    table[:known] = head[...]
    for block in range(VB):
        table[known + block] = far[block * BLK : (block + 1) * BLK, :]
    totals[...] = jnp.zeros_like(totals)

    def step(slot):
        block = source[0, 0, slot]
        place = ((block // VB) ^ column) * VB + lax.rem(block, VB)
        goal = jnp.where(slot < live, target[0, 0, slot], SPAN * VB)
        totals[goal] += jnp.dot(
            values[0, 0, slot], table[place], preferred_element_type=jnp.float32
        )

    for_slots(values.shape[2], live, step)
    for offset, out in enumerate((down2, down1, mine, up1, up2)):
        for block in range(VB):
            out[block * BLK : (block + 1) * BLK, :] = totals[offset * VB + block].astype(out.dtype)


def middle_kernel(
    mine, from_up2, from_up1, from_down1, from_down2, weight, bias, cotangent,
    output, grad_out, summed, grad, bias_part,
):
    total = mine[...]
    for part in (from_up2, from_up1, from_down1, from_down2):
        total = total + part[...].astype(jnp.float32)
    high = total.astype(jnp.bfloat16)
    low = (total - high.astype(jnp.float32)).astype(jnp.bfloat16)
    kernel = weight[...]
    pre = jnp.dot(high, kernel, preferred_element_type=jnp.float32)
    pre = pre + jnp.dot(low, kernel, preferred_element_type=jnp.float32) + bias[...]
    gate = 1.0 / (1.0 + jnp.exp(-pre))
    output[...] = (pre * gate).astype(jnp.bfloat16)
    exact = cotangent[...].astype(jnp.float32) * (gate * (1.0 + pre * (1.0 - gate)))
    grad[...] = exact.astype(jnp.bfloat16)
    grad_out[...] = lax.dot_general(
        kernel, grad[...], (((1,), (1,)), ((), ())), preferred_element_type=jnp.float32
    ).astype(jnp.bfloat16)
    summed[...] = high
    bias_part[...] = jnp.sum(exact, axis=0, keepdims=True)


def weight_kernel(summed, grad, bias_part, message):
    weight_term = lax.dot_general(
        summed[...], grad[...], (((0,), (0,)), ((), ())), preferred_element_type=jnp.float32
    )
    bias_term = bias_part[...]
    bias_high = bias_term.astype(jnp.bfloat16).astype(jnp.float32)
    lines = lax.broadcasted_iota(jnp.int32, (SLICE, LANES), 0)
    tail = jnp.zeros((SLICE, LANES), jnp.float32)
    chunks = bias_term.shape[1] // LANES
    for half, values in enumerate((bias_high, bias_term - bias_high)):
        for chunk in range(chunks):
            row = values[:, chunk * LANES : (chunk + 1) * LANES]
            tail = jnp.where(lines == half * chunks + chunk, row, tail)
    tail = tail.astype(jnp.bfloat16)
    width = weight_term.shape[1]
    for index in range(message.shape[0]):
        rows = weight_term[index * SLICE : (index + 1) * SLICE, :]
        message[index, :, :width] = rows.astype(jnp.bfloat16)
        message[index, :, width:] = tail


def backward_kernel(
    count, target, source, values, from_down2, from_down1, local, from_up1, from_up2,
    mine, near, across, far, table, totals,
):
    column = lax.axis_index("col")
    live = count[0, 0]
    for offset, part in enumerate((from_down2, from_down1, local, from_up1, from_up2)):
        for block in range(VB):
            table[offset * VB + block] = part[:, block * BLK : (block + 1) * BLK]
    totals[...] = jnp.zeros_like(totals)

    def step(slot):
        goal = jnp.where(slot < live, source[0, 0, slot], totals.shape[0] - 1)
        totals[goal] += jnp.dot(
            table[target[0, 0, slot]], values[0, 0, slot], preferred_element_type=jnp.float32
        )

    for_slots(values.shape[2], live, step)
    for relative, out in enumerate((mine, near, across, far)):
        for block in range(VB):
            out[:, block * BLK : (block + 1) * BLK] = totals[
                (column ^ relative) * VB + block
            ].astype(out.dtype)


def slice_kernel(scale, received, after, part, bias_out):
    del after
    total = jnp.sum(received[...].astype(jnp.float32), axis=0) * scale
    width = part.shape[2]
    part[...] = jnp.broadcast_to(total[:, :width].astype(jnp.bfloat16)[None], part.shape)
    chunks = width // LANES
    tail = total[:, width:]
    for chunk in range(chunks):
        bias_out[:, chunk * LANES : (chunk + 1) * LANES] = (
            tail[chunk : chunk + 1] + tail[chunks + chunk : chunks + chunk + 1]
        )


def last_kernel(mine, near, across, far, grad_inputs):
    total = mine[...]
    for part in (near, across, far):
        total = total + part[...].astype(jnp.float32)
    grad_inputs[...] = total.T.astype(jnp.bfloat16)


def join_kernel(parts, grad_weight):
    for index in range(parts.shape[0]):
        grad_weight[index * SLICE : (index + 1) * SLICE, :] = parts[index].astype(jnp.float32)


def shards(
    features, weight, bias, block_values, block_target, block_source, block_count, cotangent
):
    columns = lax.axis_size("col")
    assert columns == 4
    rows = lax.axis_size("row")
    own_rows, width = features.shape
    slots = block_values.shape[2]
    sources = columns * VB
    bf16, f32 = jnp.bfloat16, jnp.float32

    values, own, bias = call(
        stage_kernel,
        [
            jax.ShapeDtypeStruct(block_values.shape, bf16),
            jax.ShapeDtypeStruct(features.shape, bf16),
            jax.ShapeDtypeStruct((1, width), f32),
        ],
        [pltpu.SemaphoreType.DMA] * 3,
        LONG,
        [pltpu.HBM] * 3,
        "stage",
    )(block_values, features, bias[None, :])
    near = swapped(features, "col", 1)
    across = swapped(features, "col", 2)
    far = swapped(across, "col", 1)
    head = call(
        table_kernel,
        [jax.ShapeDtypeStruct((sources - VB, BLK, width), bf16)],
        [],
        LONG,
        [VMEM] * 3,
        "feature_table",
    )(own, near, across)[0]
    whole = jax.ShapeDtypeStruct((own_rows, width), bf16)
    wide = jax.ShapeDtypeStruct((own_rows, width), f32)
    mine, down2, down1, up1, up2 = call(
        forward_kernel,
        [wide] + [whole] * 4,
        [
            pltpu.VMEM((sources, BLK, width), bf16),
            pltpu.VMEM((SPAN * VB + 1, BLK, width), f32),
        ],
        2 * slots * BLK * BLK * width,
        [SMEM] * 3 + [VMEM] * 3,
        "aggregate_terms",
    )(block_count, block_target, block_source, values, head, far)

    from_up2 = shifted(down2, "row", -2)
    from_down2 = shifted(up2, "row", 2)
    from_up1 = shifted(down1, "row", -1)
    from_down1 = shifted(up1, "row", 1)
    flipped = jax.ShapeDtypeStruct((width, own_rows), bf16)
    slices = width // SLICE
    output, grad_out, summed, grad, bias_part = call(
        middle_kernel,
        [whole, flipped, whole, whole, jax.ShapeDtypeStruct((1, width), f32)],
        [],
        2 * 3 * own_rows * width * width,
        [VMEM] * 8,
        "pointwise",
    )(mine, from_up2, from_up1, from_down1, from_down2, weight, bias, cotangent)

    grad_up2 = shifted(grad_out, "row", -2)
    grad_down2 = shifted(grad_out, "row", 2)
    grad_up1 = shifted(grad_out, "row", -1)
    grad_down1 = shifted(grad_out, "row", 1)
    message = call(
        weight_kernel,
        [jax.ShapeDtypeStruct((slices, SLICE, width + LANES), bf16)],
        [],
        LONG,
        [VMEM] * 3,
        "weight_term",
    )(summed, grad, bias_part)[0]
    mine, near, across, far = call(
        backward_kernel,
        [jax.ShapeDtypeStruct((width, own_rows), f32)] + [flipped] * 3,
        [
            pltpu.VMEM((SPAN * VB, width, BLK), bf16),
            pltpu.VMEM((sources + 1, width, BLK), f32),
        ],
        LONG,
        [SMEM] * 3 + [VMEM] * 6,
        "source_terms",
    )(
        block_count, block_target, block_source, values,
        grad_down2, grad_down1, grad_out, grad_up1, grad_up2,
    )
    near = swapped(near, "col", 1)
    across = swapped(across, "col", 2)
    far = swapped(far, "col", 3)

    scale = 1.0 / math.sqrt(own_rows * rows * columns)
    everyone = ("row", "col")
    if slices == rows * columns:
        received = lax.all_to_all(message, everyone, 0, 0, tiled=True)
        part, bias_total = call(
            functools.partial(slice_kernel, scale),
            [
                jax.ShapeDtypeStruct((slices, SLICE, width), bf16),
                jax.ShapeDtypeStruct((1, width), f32),
            ],
            [],
            LONG,
            [VMEM, pl.ANY],
            "weight_slice",
        )(received, mine)
        parts = lax.all_to_all(part, everyone, 0, 0, tiled=True)
        bias_total = bias_total[0]
    else:
        total = lax.psum(message.astype(f32), everyone) * scale
        parts = total[:, :, :width].astype(bf16)
        chunks = width // LANES
        tail = total[0, : 2 * chunks, width:].reshape(2, width)
        bias_total = tail[0] + tail[1]

    grad_inputs = call(last_kernel, [whole], [], LONG, [VMEM] * 4, "source_sum")(
        mine, near, across, far
    )[0]
    grad_weight = call(
        join_kernel, [jax.ShapeDtypeStruct((width, width), f32)], [], LONG, [VMEM], "weight_join"
    )(parts)[0]
    return (output, grad_inputs, grad_weight, bias_total)


def solution(mesh):
    return jax.shard_map(
        shards,
        mesh=mesh,
        in_specs=(
            P(("row", "col"), None),
            P(),
            P(),
            P("row", "col", None, None, None),
            P("row", "col", None),
            P("row", "col", None),
            P("row", "col"),
            P(("row", "col"), None),
        ),
        out_specs=(P(("row", "col"), None), P(("row", "col"), None), P(), P()),
        check_vma=False,
    )
```

```python
import functools
import math

import jax
import jax.numpy as jnp
from jax import lax
from jax.experimental import pallas as pl
from jax.experimental.pallas import tpu as pltpu
from jax.sharding import PartitionSpec as P

BLK = 128
HALF = 2
VB = 2
SPAN = 2 * HALF + 1
TAIL = 8
SLOT_GROUP = 8
LONG = 10**11
VMEM = pltpu.VMEM
SMEM = pltpu.SMEM


def shifted(block, axis, distance):
    size = lax.axis_size(axis)
    return lax.ppermute(block, axis, [(i, (i + distance) % size) for i in range(size)])


def swapped(block, axis, bit):
    size = lax.axis_size(axis)
    return lax.ppermute(block, axis, [(i, i ^ bit) for i in range(size)])


def spec(space):
    return pl.BlockSpec(memory_space=space)


def call(body, outs, scratch, flops, spaces, name):
    return pl.pallas_call(
        body,
        out_shape=outs,
        in_specs=[spec(space) for space in spaces],
        out_specs=[spec(VMEM)] * len(outs),
        scratch_shapes=scratch,
        name=name,
        cost_estimate=pl.CostEstimate(flops=flops, bytes_accessed=2**20, transcendentals=0),
        compiler_params=pltpu.CompilerParams(vmem_limit_bytes=16 * 2**20),
    )


def for_slots(slot_total, live, step):
    for start in range(0, slot_total, SLOT_GROUP):

        @pl.when(start < live)
        def _group():
            for slot in range(start, min(start + SLOT_GROUP, slot_total)):
                step(slot)


def stage_kernel(values, own, bias, values_out, own_out, bias_out, values_sem, own_sem, bias_sem):
    copies = (
        pltpu.make_async_copy(values, values_out, values_sem),
        pltpu.make_async_copy(own, own_out, own_sem),
        pltpu.make_async_copy(bias, bias_out, bias_sem),
    )
    for copy in copies:
        copy.start()
    for copy in copies:
        copy.wait()


def table_kernel(own, near, across, head):
    for relative, part in enumerate((own, near, across)):
        for block in range(VB):
            head[relative * VB + block] = part[block * BLK : (block + 1) * BLK, :]


def forward_kernel(
    count, target, source, values, head, far,
    mine, down2, down1, up1, up2, table, totals,
):
    column = lax.axis_index("col")
    live = count[0, 0]
    known = head.shape[0]
    table[:known] = head[...]
    for block in range(VB):
        table[known + block] = far[block * BLK : (block + 1) * BLK, :]
    totals[...] = jnp.zeros_like(totals)

    def step(slot):
        block = source[0, 0, slot]
        place = ((block // VB) ^ column) * VB + lax.rem(block, VB)
        goal = jnp.where(slot < live, target[0, 0, slot], SPAN * VB)
        totals[goal] += jnp.dot(
            values[0, 0, slot], table[place], preferred_element_type=jnp.float32
        )

    for_slots(values.shape[2], live, step)
    for offset, out in enumerate((down2, down1, mine, up1, up2)):
        for block in range(VB):
            out[block * BLK : (block + 1) * BLK, :] = totals[offset * VB + block].astype(out.dtype)


def middle_kernel(
    mine, from_up2, from_up1, from_down1, from_down2, weight, bias, cotangent,
    output, grad_out, summed, grad, bias_part,
):
    total = mine[...]
    for part in (from_up2, from_up1, from_down1, from_down2):
        total = total + part[...].astype(jnp.float32)
    high = total.astype(jnp.bfloat16)
    low = (total - high.astype(jnp.float32)).astype(jnp.bfloat16)
    kernel = weight[...]
    pre = jnp.dot(high, kernel, preferred_element_type=jnp.float32)
    pre = pre + jnp.dot(low, kernel, preferred_element_type=jnp.float32) + bias[...]
    gate = 1.0 / (1.0 + jnp.exp(-pre))
    output[...] = (pre * gate).astype(jnp.bfloat16)
    exact = cotangent[...].astype(jnp.float32) * (gate * (1.0 + pre * (1.0 - gate)))
    grad[...] = exact.astype(jnp.bfloat16)
    grad_out[...] = lax.dot_general(
        kernel, grad[...], (((1,), (1,)), ((), ())), preferred_element_type=jnp.float32
    ).astype(jnp.bfloat16)
    summed[...] = high
    bias_part[...] = jnp.sum(exact, axis=0, keepdims=True)


def split_tail(row):
    high = row.astype(jnp.bfloat16).astype(jnp.float32)
    lines = lax.broadcasted_iota(jnp.int32, (TAIL, row.shape[1]), 0)
    return jnp.where(lines == 0, high, jnp.where(lines == 1, row - high, 0.0))


def weight_kernel(summed, grad, bias_part, mine, near, across, far, product):
    column = lax.axis_index("col")
    product[...] = lax.dot_general(
        summed[...], grad[...], (((0,), (0,)), ((), ())), preferred_element_type=jnp.float32
    )
    tail = split_tail(bias_part[...])
    share = mine.shape[0] - TAIL
    for relative, out in enumerate((mine, near, across, far)):
        start = pl.multiple_of((column ^ relative) * share, share)
        rows = product[pl.ds(start, share), :]
        out[...] = jnp.concatenate([rows, tail], axis=0).astype(out.dtype)


def column_sum_kernel(mine, near, across, far, message):
    total = mine[...]
    for part in (near, across, far):
        total = total + part[...].astype(jnp.float32)
    share = total.shape[0] - TAIL
    tail = split_tail(total[share : share + 1] + total[share + 1 : share + 2])
    total = jnp.concatenate([total[:share], tail], axis=0).astype(jnp.bfloat16)
    message[...] = jnp.broadcast_to(total[None], message.shape)


def backward_kernel(
    count, target, source, values, from_down2, from_down1, local, from_up1, from_up2,
    mine, near, across, far, table, totals,
):
    column = lax.axis_index("col")
    live = count[0, 0]
    for offset, part in enumerate((from_down2, from_down1, local, from_up1, from_up2)):
        for block in range(VB):
            table[offset * VB + block] = part[:, block * BLK : (block + 1) * BLK]
    totals[...] = jnp.zeros_like(totals)

    def step(slot):
        goal = jnp.where(slot < live, source[0, 0, slot], totals.shape[0] - 1)
        totals[goal] += jnp.dot(
            table[target[0, 0, slot]], values[0, 0, slot], preferred_element_type=jnp.float32
        )

    for_slots(values.shape[2], live, step)
    for relative, out in enumerate((mine, near, across, far)):
        for block in range(VB):
            out[:, block * BLK : (block + 1) * BLK] = totals[
                (column ^ relative) * VB + block
            ].astype(out.dtype)


def row_sum_kernel(scale, received, after, part, bias_out):
    del after
    total = jnp.sum(received[...].astype(jnp.float32), axis=0) * scale
    share = part.shape[0]
    part[...] = total[:share].astype(part.dtype)
    bias_out[...] = total[share : share + 1] + total[share + 1 : share + 2]


def last_kernel(mine, near, across, far, grad_inputs):
    total = mine[...]
    for part in (near, across, far):
        total = total + part[...].astype(jnp.float32)
    grad_inputs[...] = total.T.astype(jnp.bfloat16)


def join_kernel(own, near, across, far, grad_weight):
    column = lax.axis_index("col")
    share = own.shape[0]
    for relative, part in enumerate((own, near, across, far)):
        start = pl.multiple_of((column ^ relative) * share, share)
        grad_weight[pl.ds(start, share), :] = part[...].astype(jnp.float32)


def shards(
    features, weight, bias, block_values, block_target, block_source, block_count, cotangent
):
    columns = lax.axis_size("col")
    assert columns == 4
    rows = lax.axis_size("row")
    own_rows, width = features.shape
    slots = block_values.shape[2]
    sources = columns * VB
    bf16, f32 = jnp.bfloat16, jnp.float32

    values, own, bias = call(
        stage_kernel,
        [
            jax.ShapeDtypeStruct(block_values.shape, bf16),
            jax.ShapeDtypeStruct(features.shape, bf16),
            jax.ShapeDtypeStruct((1, width), f32),
        ],
        [pltpu.SemaphoreType.DMA] * 3,
        LONG,
        [pltpu.HBM] * 3,
        "stage",
    )(block_values, features, bias[None, :])
    near = swapped(features, "col", 1)
    across = swapped(features, "col", 2)
    far = swapped(across, "col", 1)
    head = call(
        table_kernel,
        [jax.ShapeDtypeStruct((sources - VB, BLK, width), bf16)],
        [],
        LONG,
        [VMEM] * 3,
        "feature_table",
    )(own, near, across)[0]
    whole = jax.ShapeDtypeStruct((own_rows, width), bf16)
    wide = jax.ShapeDtypeStruct((own_rows, width), f32)
    mine, down2, down1, up1, up2 = call(
        forward_kernel,
        [wide] + [whole] * 4,
        [
            pltpu.VMEM((sources, BLK, width), bf16),
            pltpu.VMEM((SPAN * VB + 1, BLK, width), f32),
        ],
        2 * slots * BLK * BLK * width,
        [SMEM] * 3 + [VMEM] * 3,
        "aggregate_terms",
    )(block_count, block_target, block_source, values, head, far)

    from_up2 = shifted(down2, "row", -2)
    from_down2 = shifted(up2, "row", 2)
    from_up1 = shifted(down1, "row", -1)
    from_down1 = shifted(up1, "row", 1)
    flipped = jax.ShapeDtypeStruct((width, own_rows), bf16)
    output, grad_out, summed, grad, bias_part = call(
        middle_kernel,
        [whole, flipped, whole, whole, jax.ShapeDtypeStruct((1, width), f32)],
        [],
        2 * 3 * own_rows * width * width,
        [VMEM] * 8,
        "pointwise",
    )(mine, from_up2, from_up1, from_down1, from_down2, weight, bias, cotangent)

    grad_up2 = shifted(grad_out, "row", -2)
    grad_down2 = shifted(grad_out, "row", 2)
    grad_up1 = shifted(grad_out, "row", -1)
    grad_down1 = shifted(grad_out, "row", 1)
    share = width // columns
    packed = (share + TAIL, width)
    weight_mine, weight_near, weight_across, weight_far = call(
        weight_kernel,
        [jax.ShapeDtypeStruct(packed, f32)] + [jax.ShapeDtypeStruct(packed, bf16)] * 3,
        [pltpu.VMEM((width, width), f32)],
        LONG,
        [VMEM] * 3,
        "weight_term",
    )(summed, grad, bias_part)
    message = call(
        column_sum_kernel,
        [jax.ShapeDtypeStruct((rows,) + packed, bf16)],
        [],
        LONG,
        [VMEM] * 4,
        "weight_column_sum",
    )(
        weight_mine,
        swapped(weight_near, "col", 1),
        swapped(weight_across, "col", 2),
        swapped(weight_far, "col", 3),
    )[0]
    mine, near, across, far = call(
        backward_kernel,
        [jax.ShapeDtypeStruct((width, own_rows), f32)] + [flipped] * 3,
        [
            pltpu.VMEM((SPAN * VB, width, BLK), bf16),
            pltpu.VMEM((sources + 1, width, BLK), f32),
        ],
        LONG,
        [SMEM] * 3 + [VMEM] * 6,
        "source_terms",
    )(
        block_count, block_target, block_source, values,
        grad_down2, grad_down1, grad_out, grad_up1, grad_up2,
    )
    near = swapped(near, "col", 1)
    across = swapped(across, "col", 2)
    far = swapped(far, "col", 3)

    scale = 1.0 / math.sqrt(own_rows * rows * columns)
    if rows > 8:
        received = lax.psum(message[:1].astype(f32), "row")
    else:
        received = lax.all_to_all(message, "row", 0, 0, tiled=True)
    part, bias_total = call(
        functools.partial(row_sum_kernel, scale),
        [jax.ShapeDtypeStruct((share, width), bf16), jax.ShapeDtypeStruct((1, width), f32)],
        [],
        LONG,
        [VMEM, pl.ANY],
        "weight_row_sum",
    )(received, mine)
    parts = [part] + [swapped(part, "col", bit) for bit in (1, 2, 3)]

    grad_inputs = call(last_kernel, [whole], [], LONG, [VMEM] * 4, "source_sum")(
        mine, near, across, far
    )[0]
    grad_weight = call(
        join_kernel, [jax.ShapeDtypeStruct((width, width), f32)], [], LONG, [VMEM] * 4, "weight_join"
    )(*parts)[0]
    return (output, grad_inputs, grad_weight, bias_total[0])


def solution(mesh):
    return jax.shard_map(
        shards,
        mesh=mesh,
        in_specs=(
            P(("row", "col"), None),
            P(),
            P(),
            P("row", "col", None, None, None),
            P("row", "col", None),
            P("row", "col", None),
            P("row", "col"),
            P(("row", "col"), None),
        ),
        out_specs=(P(("row", "col"), None), P(("row", "col"), None), P(), P()),
        check_vma=False,
    )
```

```python
import functools
import math

import jax
import jax.numpy as jnp
from jax import lax
from jax.experimental import pallas as pl
from jax.experimental.pallas import tpu as pltpu
from jax.sharding import PartitionSpec as P

BLK = 128
HALF = 2
VB = 2
SPAN = 2 * HALF + 1
TAIL = 8
FORWARD = ((2, None), (1, None), (-2, None), (-1, None))
BACKWARD = ((2, None), (1, None), (-2, None), (-1, None))
SLOT_GROUP = 32
LONG = 10**11
VMEM = pltpu.VMEM
SMEM = pltpu.SMEM


def offset_at(route, row):
    reach, phase = route
    if phase is None:
        return reach, -reach
    toward = reach * (1 - 2 * lax.rem(row // reach + phase, 2))
    return toward, toward


def routed(block, route):
    size = lax.axis_size("row")
    reach, phase = route
    pairs = []
    for i in range(size):
        if phase is None:
            pairs.append((i, (i + reach) % size))
        else:
            pairs.append((i, (i + reach * (1 - 2 * ((i // reach + phase) % 2))) % size))
    return lax.ppermute(block, "row", pairs)


def swapped(block, axis, bit):
    size = lax.axis_size(axis)
    return lax.ppermute(block, axis, [(i, i ^ bit) for i in range(size)])


def spec(space):
    return pl.BlockSpec(memory_space=space)


def call(body, outs, scratch, flops, spaces, name):
    return pl.pallas_call(
        body,
        out_shape=outs,
        in_specs=[spec(space) for space in spaces],
        out_specs=[spec(VMEM)] * len(outs),
        scratch_shapes=scratch,
        name=name,
        cost_estimate=pl.CostEstimate(flops=flops, bytes_accessed=2**20, transcendentals=0),
        compiler_params=pltpu.CompilerParams(vmem_limit_bytes=16 * 2**20),
    )


def for_slots(slot_total, live, step):
    for start in range(0, slot_total, SLOT_GROUP):

        @pl.when(start < live)
        def _group():
            for slot in range(start, min(start + SLOT_GROUP, slot_total)):
                step(slot)


def stage_kernel(values, own, bias, values_out, own_out, bias_out, values_sem, own_sem, bias_sem):
    copies = (
        pltpu.make_async_copy(values, values_out, values_sem),
        pltpu.make_async_copy(own, own_out, own_sem),
        pltpu.make_async_copy(bias, bias_out, bias_sem),
    )
    for copy in copies:
        copy.start()
    for copy in copies:
        copy.wait()


def table_kernel(own, near, across, head):
    for relative, part in enumerate((own, near, across)):
        for block in range(VB):
            head[relative * VB + block] = part[block * BLK : (block + 1) * BLK, :]


def forward_kernel(
    count, target, source, values, head, far,
    mine, first, second, third, fourth, table, totals,
):
    column = lax.axis_index("col")
    live = count[0, 0]
    known = head.shape[0]
    table[:known] = head[...]
    for block in range(VB):
        table[known + block] = far[block * BLK : (block + 1) * BLK, :]
    totals[...] = jnp.zeros_like(totals)

    def step(slot):
        block = source[0, 0, slot]
        place = ((block // VB) ^ column) * VB + lax.rem(block, VB)
        goal = jnp.where(slot < live, target[0, 0, slot], SPAN * VB)
        totals[goal] += jnp.dot(
            values[0, 0, slot], table[place], preferred_element_type=jnp.float32
        )

    for_slots(values.shape[2], live, step)
    row = lax.axis_index("row")
    offsets = [0] + [offset_at(route, row)[0] for route in FORWARD]
    for offset, out in zip(offsets, (mine, first, second, third, fourth)):
        for block in range(VB):
            out[block * BLK : (block + 1) * BLK, :] = totals[
                (HALF + offset) * VB + block
            ].astype(out.dtype)


def middle_kernel(
    mine, first, second, third, fourth, weight, bias, cotangent,
    output, grad_out, summed, grad, bias_part,
):
    total = mine[...]
    for part in (first, second, third, fourth):
        total = total + part[...].astype(jnp.float32)
    high = total.astype(jnp.bfloat16)
    low = (total - high.astype(jnp.float32)).astype(jnp.bfloat16)
    kernel = weight[...]
    pre = jnp.dot(high, kernel, preferred_element_type=jnp.float32)
    pre = pre + jnp.dot(low, kernel, preferred_element_type=jnp.float32) + bias[...]
    gate = 1.0 / (1.0 + jnp.exp(-pre))
    output[...] = (pre * gate).astype(jnp.bfloat16)
    exact = cotangent[...].astype(jnp.float32) * (gate * (1.0 + pre * (1.0 - gate)))
    grad[...] = exact.astype(jnp.bfloat16)
    grad_out[...] = lax.dot_general(
        kernel, grad[...], (((1,), (1,)), ((), ())), preferred_element_type=jnp.float32
    ).astype(jnp.bfloat16)
    summed[...] = high
    bias_part[...] = jnp.sum(exact, axis=0, keepdims=True)


def split_tail(row):
    high = row.astype(jnp.bfloat16).astype(jnp.float32)
    lines = lax.broadcasted_iota(jnp.int32, (TAIL, row.shape[1]), 0)
    return jnp.where(lines == 0, high, jnp.where(lines == 1, row - high, 0.0))


def weight_kernel(summed, grad, bias_part, mine, near, across, far, product):
    column = lax.axis_index("col")
    product[...] = lax.dot_general(
        summed[...], grad[...], (((0,), (0,)), ((), ())), preferred_element_type=jnp.float32
    )
    tail = split_tail(bias_part[...])
    share = mine.shape[0] - TAIL
    for relative, out in enumerate((mine, near, across, far)):
        start = pl.multiple_of((column ^ relative) * share, share)
        rows = product[pl.ds(start, share), :]
        out[...] = jnp.concatenate([rows, tail], axis=0).astype(out.dtype)


def column_sum_kernel(mine, near, across, far, message):
    total = mine[...]
    for part in (near, across, far):
        total = total + part[...].astype(jnp.float32)
    share = total.shape[0] - TAIL
    tail = split_tail(total[share : share + 1] + total[share + 1 : share + 2])
    total = jnp.concatenate([total[:share], tail], axis=0).astype(jnp.bfloat16)
    message[...] = jnp.broadcast_to(total[None], message.shape)


def backward_kernel(
    count, target, source, values, local, first, second, third, fourth,
    mine, near, across, far, table, totals,
):
    column = lax.axis_index("col")
    live = count[0, 0]
    row = lax.axis_index("row")
    offsets = [0] + [offset_at(route, row)[1] for route in BACKWARD]
    for offset, part in zip(offsets, (local, first, second, third, fourth)):
        for block in range(VB):
            table[(HALF + offset) * VB + block] = part[:, block * BLK : (block + 1) * BLK]
    totals[...] = jnp.zeros_like(totals)

    def step(slot):
        goal = jnp.where(slot < live, source[0, 0, slot], totals.shape[0] - 1)
        totals[goal] += jnp.dot(
            table[target[0, 0, slot]], values[0, 0, slot], preferred_element_type=jnp.float32
        )

    for_slots(values.shape[2], live, step)
    for relative, out in enumerate((mine, near, across, far)):
        for block in range(VB):
            out[:, block * BLK : (block + 1) * BLK] = totals[
                (column ^ relative) * VB + block
            ].astype(out.dtype)


def row_sum_kernel(scale, received, after, part, bias_out):
    del after
    total = jnp.sum(received[...].astype(jnp.float32), axis=0) * scale
    share = part.shape[0]
    part[...] = total[:share].astype(part.dtype)
    bias_out[...] = total[share : share + 1] + total[share + 1 : share + 2]


def last_kernel(mine, near, across, far, grad_inputs):
    total = mine[...]
    for part in (near, across, far):
        total = total + part[...].astype(jnp.float32)
    grad_inputs[...] = total.T.astype(jnp.bfloat16)


def join_kernel(
    own, near, across, far, bias_in, output_in, source_in, grad_weight, bias_out, output, grad_inputs
):
    column = lax.axis_index("col")
    share = own.shape[0]
    for relative, part in enumerate((own, near, across, far)):
        start = pl.multiple_of((column ^ relative) * share, share)
        grad_weight[pl.ds(start, share), :] = part[...].astype(jnp.float32)
    bias_out[...] = bias_in[...]
    output[...] = output_in[...]
    grad_inputs[...] = source_in[...]


def shards(
    features, weight, bias, block_values, block_target, block_source, block_count, cotangent
):
    columns = lax.axis_size("col")
    assert columns == 4
    rows = lax.axis_size("row")
    own_rows, width = features.shape
    slots = block_values.shape[2]
    sources = columns * VB
    bf16, f32 = jnp.bfloat16, jnp.float32

    values, own, bias = call(
        stage_kernel,
        [
            jax.ShapeDtypeStruct(block_values.shape, bf16),
            jax.ShapeDtypeStruct(features.shape, bf16),
            jax.ShapeDtypeStruct((1, width), f32),
        ],
        [pltpu.SemaphoreType.DMA] * 3,
        LONG,
        [pltpu.HBM] * 3,
        "stage",
    )(block_values, features, bias[None, :])
    near = swapped(features, "col", 1)
    across = swapped(features, "col", 2)
    far = swapped(across, "col", 1)
    head = call(
        table_kernel,
        [jax.ShapeDtypeStruct((sources - VB, BLK, width), bf16)],
        [],
        LONG,
        [VMEM] * 3,
        "feature_table",
    )(own, near, across)[0]
    whole = jax.ShapeDtypeStruct((own_rows, width), bf16)
    wide = jax.ShapeDtypeStruct((own_rows, width), f32)
    mine, *leaving = call(
        forward_kernel,
        [wide] + [whole] * 4,
        [
            pltpu.VMEM((sources, BLK, width), bf16),
            pltpu.VMEM((SPAN * VB + 1, BLK, width), f32),
        ],
        2 * slots * BLK * BLK * width,
        [SMEM] * 3 + [VMEM] * 3,
        "aggregate_terms",
    )(block_count, block_target, block_source, values, head, far)

    arrived = [routed(block, route) for block, route in zip(leaving, FORWARD)]
    flipped = jax.ShapeDtypeStruct((width, own_rows), bf16)
    output, grad_out, summed, grad, bias_part = call(
        middle_kernel,
        [whole, flipped, whole, whole, jax.ShapeDtypeStruct((1, width), f32)],
        [],
        2 * 3 * own_rows * width * width,
        [VMEM] * 8,
        "pointwise",
    )(mine, *arrived, weight, bias, cotangent)

    arrived = [routed(grad_out, route) for route in BACKWARD]
    share = width // columns
    packed = (share + TAIL, width)
    weight_mine, weight_near, weight_across, weight_far = call(
        weight_kernel,
        [jax.ShapeDtypeStruct(packed, f32)] + [jax.ShapeDtypeStruct(packed, bf16)] * 3,
        [pltpu.VMEM((width, width), f32)],
        LONG,
        [VMEM] * 3,
        "weight_term",
    )(summed, grad, bias_part)
    message = call(
        column_sum_kernel,
        [jax.ShapeDtypeStruct((rows,) + packed, bf16)],
        [],
        LONG,
        [VMEM] * 4,
        "weight_column_sum",
    )(
        weight_mine,
        swapped(weight_near, "col", 1),
        swapped(weight_across, "col", 2),
        swapped(weight_far, "col", 3),
    )[0]
    mine, near, across, far = call(
        backward_kernel,
        [jax.ShapeDtypeStruct((width, own_rows), f32)] + [flipped] * 3,
        [
            pltpu.VMEM((SPAN * VB, width, BLK), bf16),
            pltpu.VMEM((sources + 1, width, BLK), f32),
        ],
        LONG,
        [SMEM] * 3 + [VMEM] * 6,
        "source_terms",
    )(
        block_count, block_target, block_source, values,
        grad_out, *arrived,
    )
    near = swapped(near, "col", 1)
    across = swapped(across, "col", 2)
    far = swapped(far, "col", 3)

    scale = 1.0 / math.sqrt(own_rows * rows * columns)
    if rows > 8:
        received = lax.psum(message[:1].astype(f32), "row")
    else:
        received = lax.all_to_all(message, "row", 0, 0, tiled=True)
    part, bias_total = call(
        functools.partial(row_sum_kernel, scale),
        [jax.ShapeDtypeStruct((share, width), bf16), jax.ShapeDtypeStruct((1, width), f32)],
        [],
        LONG,
        [VMEM, pl.ANY],
        "weight_row_sum",
    )(received, mine)
    parts = [part] + [swapped(part, "col", bit) for bit in (1, 2, 3)]

    grad_inputs = call(last_kernel, [whole], [], LONG, [VMEM] * 4, "source_sum")(
        mine, near, across, far
    )[0]
    grad_weight, bias_total, output, grad_inputs = call(
        join_kernel,
        [
            jax.ShapeDtypeStruct((width, width), f32),
            jax.ShapeDtypeStruct((1, width), f32),
            whole,
            whole,
        ],
        [],
        LONG,
        [VMEM] * 7,
        "results",
    )(*parts, bias_total, output, grad_inputs)
    return (output, grad_inputs, grad_weight, bias_total[0])


def solution(mesh):
    return jax.shard_map(
        shards,
        mesh=mesh,
        in_specs=(
            P(("row", "col"), None),
            P(),
            P(),
            P("row", "col", None, None, None),
            P("row", "col", None),
            P("row", "col", None),
            P("row", "col"),
            P(("row", "col"), None),
        ),
        out_specs=(P(("row", "col"), None), P(("row", "col"), None), P(), P()),
        check_vma=False,
    )
```

```python
import functools
import math

import jax
import jax.numpy as jnp
from jax import lax
from jax.experimental import pallas as pl
from jax.experimental.pallas import tpu as pltpu
from jax.sharding import PartitionSpec as P

BLK = 128
HALF = 2
VB = 2
SPAN = 2 * HALF + 1
TAIL = 8
FORWARD = ((2, None), (1, None), (-2, None), (-1, None))
BACKWARD = ((-2, None), (-1, None), (1, None), (2, None))
SLOT_GROUP = 32
LONG = 10**11
VMEM = pltpu.VMEM
SMEM = pltpu.SMEM


def offset_at(route, row):
    reach, phase = route
    if phase is None:
        return reach, -reach
    toward = reach * (1 - 2 * lax.rem(row // reach + phase, 2))
    return toward, toward


def routed(block, route):
    size = lax.axis_size("row")
    reach, phase = route
    pairs = []
    for i in range(size):
        if phase is None:
            pairs.append((i, (i + reach) % size))
        else:
            pairs.append((i, (i + reach * (1 - 2 * ((i // reach + phase) % 2))) % size))
    return lax.ppermute(block, "row", pairs)


def swapped(block, axis, bit):
    size = lax.axis_size(axis)
    return lax.ppermute(block, axis, [(i, i ^ bit) for i in range(size)])


def spec(space):
    return pl.BlockSpec(memory_space=space)


def call(body, outs, scratch, flops, spaces, name):
    return pl.pallas_call(
        body,
        out_shape=outs,
        in_specs=[spec(space) for space in spaces],
        out_specs=[spec(VMEM)] * len(outs),
        scratch_shapes=scratch,
        name=name,
        cost_estimate=pl.CostEstimate(flops=flops, bytes_accessed=2**20, transcendentals=0),
        compiler_params=pltpu.CompilerParams(vmem_limit_bytes=16 * 2**20),
    )


def for_slots(slot_total, live, step):
    for start in range(0, slot_total, SLOT_GROUP):

        @pl.when(start < live)
        def _group():
            for slot in range(start, min(start + SLOT_GROUP, slot_total)):
                step(slot)


def stage_kernel(values, own, bias, values_out, own_out, bias_out, values_sem, own_sem, bias_sem):
    copies = (
        pltpu.make_async_copy(values, values_out, values_sem),
        pltpu.make_async_copy(own, own_out, own_sem),
        pltpu.make_async_copy(bias, bias_out, bias_sem),
    )
    for copy in copies:
        copy.start()
    for copy in copies:
        copy.wait()


def table_kernel(own, near, across, head):
    for relative, part in enumerate((own, near, across)):
        for block in range(VB):
            head[relative * VB + block] = part[block * BLK : (block + 1) * BLK, :]


def forward_kernel(
    count, target, source, values, head, far,
    mine, first, second, third, fourth, table, totals,
):
    column = lax.axis_index("col")
    live = count[0, 0]
    known = head.shape[0]
    table[:known] = head[...]
    for block in range(VB):
        table[known + block] = far[block * BLK : (block + 1) * BLK, :]
    totals[...] = jnp.zeros_like(totals)

    def step(slot):
        block = source[0, 0, slot]
        place = ((block // VB) ^ column) * VB + lax.rem(block, VB)
        goal = jnp.where(slot < live, target[0, 0, slot], SPAN * VB)
        totals[goal] += jnp.dot(
            values[0, 0, slot], table[place], preferred_element_type=jnp.float32
        )

    for_slots(values.shape[2], live, step)
    row = lax.axis_index("row")
    offsets = [0] + [offset_at(route, row)[0] for route in FORWARD]
    for offset, out in zip(offsets, (mine, first, second, third, fourth)):
        for block in range(VB):
            out[block * BLK : (block + 1) * BLK, :] = totals[
                (HALF + offset) * VB + block
            ].astype(out.dtype)


def middle_kernel(
    mine, first, second, third, fourth, weight, bias, cotangent,
    output, grad_out, summed, grad, bias_part,
):
    total = mine[...]
    for part in (first, second, third, fourth):
        total = total + part[...].astype(jnp.float32)
    high = total.astype(jnp.bfloat16)
    low = (total - high.astype(jnp.float32)).astype(jnp.bfloat16)
    kernel = weight[...]
    pre = jnp.dot(high, kernel, preferred_element_type=jnp.float32)
    pre = pre + jnp.dot(low, kernel, preferred_element_type=jnp.float32) + bias[...]
    gate = 1.0 / (1.0 + jnp.exp(-pre))
    output[...] = (pre * gate).astype(jnp.bfloat16)
    exact = cotangent[...].astype(jnp.float32) * (gate * (1.0 + pre * (1.0 - gate)))
    grad[...] = exact.astype(jnp.bfloat16)
    grad_out[...] = lax.dot_general(
        kernel, grad[...], (((1,), (1,)), ((), ())), preferred_element_type=jnp.float32
    ).astype(jnp.bfloat16)
    summed[...] = high
    bias_part[...] = jnp.sum(exact, axis=0, keepdims=True)


def split_tail(row):
    high = row.astype(jnp.bfloat16).astype(jnp.float32)
    lines = lax.broadcasted_iota(jnp.int32, (TAIL, row.shape[1]), 0)
    return jnp.where(lines == 0, high, jnp.where(lines == 1, row - high, 0.0))


def weight_kernel(summed, grad, bias_part, mine, near, across, far, product):
    column = lax.axis_index("col")
    product[...] = lax.dot_general(
        summed[...], grad[...], (((0,), (0,)), ((), ())), preferred_element_type=jnp.float32
    )
    tail = split_tail(bias_part[...])
    share = mine.shape[0] - TAIL
    for relative, out in enumerate((mine, near, across, far)):
        start = pl.multiple_of((column ^ relative) * share, share)
        rows = product[pl.ds(start, share), :]
        out[...] = jnp.concatenate([rows, tail], axis=0).astype(out.dtype)


def column_sum_kernel(mine, near, across, far, message):
    total = mine[...]
    for part in (near, across, far):
        total = total + part[...].astype(jnp.float32)
    share = total.shape[0] - TAIL
    tail = split_tail(total[share : share + 1] + total[share + 1 : share + 2])
    total = jnp.concatenate([total[:share], tail], axis=0).astype(jnp.bfloat16)
    message[...] = jnp.broadcast_to(total[None], message.shape)


def backward_kernel(
    count, target, source, values, local, first, second, third, fourth,
    mine, across, leaving, table, totals,
):
    column = lax.axis_index("col")
    live = count[0, 0]
    row = lax.axis_index("row")
    offsets = [0] + [offset_at(route, row)[1] for route in BACKWARD]
    for offset, part in zip(offsets, (local, first, second, third, fourth)):
        for block in range(VB):
            table[(HALF + offset) * VB + block] = part[:, block * BLK : (block + 1) * BLK]
    totals[...] = jnp.zeros_like(totals)

    def step(slot):
        goal = jnp.where(slot < live, source[0, 0, slot], totals.shape[0] - 1)
        totals[goal] += jnp.dot(
            table[target[0, 0, slot]], values[0, 0, slot], preferred_element_type=jnp.float32
        )

    for_slots(values.shape[2], live, step)
    outs = (mine, leaving.at[0], across, leaving.at[1])
    for relative, out in enumerate(outs):
        for block in range(VB):
            out[:, block * BLK : (block + 1) * BLK] = totals[
                (column ^ relative) * VB + block
            ].astype(out.dtype)


def source_pair_kernel(mine, across, arrived, kept, leaving):
    kept[...] = mine[...] + arrived[0].astype(jnp.float32)
    leaving[...] = (across[...] + arrived[1].astype(jnp.float32)).astype(leaving.dtype)


def row_sum_kernel(scale, received, after, part, bias_out):
    del after
    total = jnp.sum(received[...].astype(jnp.float32), axis=0) * scale
    share = part.shape[0]
    part[...] = total[:share].astype(part.dtype)
    bias_out[...] = total[share : share + 1] + total[share + 1 : share + 2]


def last_kernel(mine, arrived, output_in, bias_in, grad_inputs, output, bias_out):
    total = mine[...] + arrived[...].astype(jnp.float32)
    grad_inputs[...] = total.T.astype(jnp.bfloat16)
    output[...] = output_in[...]
    bias_out[...] = bias_in[...]


def join_kernel(own, near, across, far, grad_weight):
    column = lax.axis_index("col")
    share = own.shape[0]
    for relative, part in enumerate((own, near, across, far)):
        start = pl.multiple_of((column ^ relative) * share, share)
        grad_weight[pl.ds(start, share), :] = part[...].astype(jnp.float32)


def shards(
    features, weight, bias, block_values, block_target, block_source, block_count, cotangent
):
    columns = lax.axis_size("col")
    assert columns == 4
    rows = lax.axis_size("row")
    own_rows, width = features.shape
    slots = block_values.shape[2]
    sources = columns * VB
    bf16, f32 = jnp.bfloat16, jnp.float32

    values, own, bias = call(
        stage_kernel,
        [
            jax.ShapeDtypeStruct(block_values.shape, bf16),
            jax.ShapeDtypeStruct(features.shape, bf16),
            jax.ShapeDtypeStruct((1, width), f32),
        ],
        [pltpu.SemaphoreType.DMA] * 3,
        LONG,
        [pltpu.HBM] * 3,
        "stage",
    )(block_values, features, bias[None, :])
    near = swapped(features, "col", 1)
    across = swapped(features, "col", 2)
    far = swapped(across, "col", 1)
    head = call(
        table_kernel,
        [jax.ShapeDtypeStruct((sources - VB, BLK, width), bf16)],
        [],
        LONG,
        [VMEM] * 3,
        "feature_table",
    )(own, near, across)[0]
    whole = jax.ShapeDtypeStruct((own_rows, width), bf16)
    wide = jax.ShapeDtypeStruct((own_rows, width), f32)
    mine, *leaving = call(
        forward_kernel,
        [wide] + [whole] * 4,
        [
            pltpu.VMEM((sources, BLK, width), bf16),
            pltpu.VMEM((SPAN * VB + 1, BLK, width), f32),
        ],
        2 * slots * BLK * BLK * width,
        [SMEM] * 3 + [VMEM] * 3,
        "aggregate_terms",
    )(block_count, block_target, block_source, values, head, far)

    arrived = [routed(block, route) for block, route in zip(leaving, FORWARD)]
    flipped = jax.ShapeDtypeStruct((width, own_rows), bf16)
    output, grad_out, summed, grad, bias_part = call(
        middle_kernel,
        [whole, flipped, whole, whole, jax.ShapeDtypeStruct((1, width), f32)],
        [],
        2 * 3 * own_rows * width * width,
        [VMEM] * 8,
        "pointwise",
    )(mine, *arrived, weight, bias, cotangent)

    arrived = [routed(grad_out, route) for route in BACKWARD]
    share = width // columns
    packed = (share + TAIL, width)
    weight_mine, weight_near, weight_across, weight_far = call(
        weight_kernel,
        [jax.ShapeDtypeStruct(packed, f32)] + [jax.ShapeDtypeStruct(packed, bf16)] * 3,
        [pltpu.VMEM((width, width), f32)],
        LONG,
        [VMEM] * 3,
        "weight_term",
    )(summed, grad, bias_part)
    message = call(
        column_sum_kernel,
        [jax.ShapeDtypeStruct((rows,) + packed, bf16)],
        [],
        LONG,
        [VMEM] * 4,
        "weight_column_sum",
    )(
        weight_mine,
        swapped(weight_near, "col", 1),
        swapped(weight_across, "col", 2),
        swapped(weight_far, "col", 3),
    )[0]
    tall = jax.ShapeDtypeStruct((width, own_rows), f32)
    mine, across, leaving = call(
        backward_kernel,
        [tall, tall, jax.ShapeDtypeStruct((2, width, own_rows), bf16)],
        [
            pltpu.VMEM((SPAN * VB, width, BLK), bf16),
            pltpu.VMEM((sources + 1, width, BLK), f32),
        ],
        LONG,
        [SMEM] * 3 + [VMEM] * 6,
        "source_terms",
    )(
        block_count, block_target, block_source, values,
        grad_out, *arrived,
    )
    kept, leaving = call(
        source_pair_kernel, [tall, flipped], [], 0, [VMEM] * 3, "source_pair_sum"
    )(mine, across, swapped(leaving, "col", 1))
    across = swapped(leaving, "col", 2)

    scale = 1.0 / math.sqrt(own_rows * rows * columns)
    if rows > 8:
        received = lax.psum(message[:1].astype(f32), "row")
    else:
        received = lax.all_to_all(message, "row", 0, 0, tiled=True)
    part, bias_total = call(
        functools.partial(row_sum_kernel, scale),
        [jax.ShapeDtypeStruct((share, width), bf16), jax.ShapeDtypeStruct((1, width), f32)],
        [],
        LONG,
        [VMEM, pl.ANY],
        "weight_row_sum",
    )(received, mine)
    parts = [part] + [swapped(part, "col", bit) for bit in (1, 2, 3)]

    grad_inputs, output, bias_total = call(
        last_kernel,
        [whole, whole, jax.ShapeDtypeStruct((1, width), f32)],
        [],
        LONG,
        [VMEM] * 4,
        "source_sum",
    )(kept, across, output, bias_total)
    grad_weight = call(
        join_kernel, [jax.ShapeDtypeStruct((width, width), f32)], [], LONG, [VMEM] * 4, "weight_join"
    )(*parts)[0]
    return (output, grad_inputs, grad_weight, bias_total[0])


def solution(mesh):
    return jax.shard_map(
        shards,
        mesh=mesh,
        in_specs=(
            P(("row", "col"), None),
            P(),
            P(),
            P("row", "col", None, None, None),
            P("row", "col", None),
            P("row", "col", None),
            P("row", "col"),
            P(("row", "col"), None),
        ),
        out_specs=(P(("row", "col"), None), P(("row", "col"), None), P(), P()),
        check_vma=False,
    )
```

```python
import functools
import math

import jax
import jax.numpy as jnp
from jax import lax
from jax.experimental import pallas as pl
from jax.experimental.pallas import tpu as pltpu
from jax.sharding import PartitionSpec as P

BLK = 128
HALF = 2
VB = 2
SPAN = 2 * HALF + 1
TAIL = 8
FORWARD = ((1, None), (2, None), (-2, None), (-1, None))
BACKWARD = ((-1, None), (-2, None), (1, None), (2, None))
SLOT_GROUP = 32
LONG = 10**11
VMEM = pltpu.VMEM
SMEM = pltpu.SMEM


def offset_at(route, row):
    reach, phase = route
    if phase is None:
        return reach, -reach
    toward = reach * (1 - 2 * lax.rem(row // reach + phase, 2))
    return toward, toward


def routed(block, route):
    size = lax.axis_size("row")
    reach, phase = route
    pairs = []
    for i in range(size):
        if phase is None:
            pairs.append((i, (i + reach) % size))
        else:
            pairs.append((i, (i + reach * (1 - 2 * ((i // reach + phase) % 2))) % size))
    return lax.ppermute(block, "row", pairs)


def swapped(block, axis, bit):
    size = lax.axis_size(axis)
    return lax.ppermute(block, axis, [(i, i ^ bit) for i in range(size)])


def spec(space):
    return pl.BlockSpec(memory_space=space)


def call(body, outs, scratch, flops, spaces, name):
    return pl.pallas_call(
        body,
        out_shape=outs,
        in_specs=[spec(space) for space in spaces],
        out_specs=[spec(VMEM)] * len(outs),
        scratch_shapes=scratch,
        name=name,
        cost_estimate=pl.CostEstimate(flops=flops, bytes_accessed=2**20, transcendentals=0),
        compiler_params=pltpu.CompilerParams(vmem_limit_bytes=16 * 2**20),
    )


def for_slots(slot_total, live, step):
    for start in range(0, slot_total, SLOT_GROUP):

        @pl.when(start < live)
        def _group():
            for slot in range(start, min(start + SLOT_GROUP, slot_total)):
                step(slot)


def stage_kernel(values, own, bias, values_out, own_out, bias_out, values_sem, own_sem, bias_sem):
    copies = (
        pltpu.make_async_copy(values, values_out, values_sem),
        pltpu.make_async_copy(own, own_out, own_sem),
        pltpu.make_async_copy(bias, bias_out, bias_sem),
    )
    for copy in copies:
        copy.start()
    for copy in copies:
        copy.wait()


def table_kernel(own, near, across, head):
    for relative, part in enumerate((own, near, across)):
        for block in range(VB):
            head[relative * VB + block] = part[block * BLK : (block + 1) * BLK, :]


def forward_kernel(
    count, target, source, values, head, far,
    mine, first, second, third, fourth, table, totals,
):
    column = lax.axis_index("col")
    live = count[0, 0]
    known = head.shape[0]
    table[:known] = head[...]
    for block in range(VB):
        table[known + block] = far[block * BLK : (block + 1) * BLK, :]
    totals[...] = jnp.zeros_like(totals)

    def step(slot):
        block = source[0, 0, slot]
        place = ((block // VB) ^ column) * VB + lax.rem(block, VB)
        goal = jnp.where(slot < live, target[0, 0, slot], SPAN * VB)
        totals[goal] += jnp.dot(
            values[0, 0, slot], table[place], preferred_element_type=jnp.float32
        )

    for_slots(values.shape[2], live, step)
    row = lax.axis_index("row")
    offsets = [0] + [offset_at(route, row)[0] for route in FORWARD]
    for offset, out in zip(offsets, (mine, first, second, third, fourth)):
        for block in range(VB):
            out[block * BLK : (block + 1) * BLK, :] = totals[
                (HALF + offset) * VB + block
            ].astype(out.dtype)


def middle_kernel(
    mine, first, second, third, fourth, weight, bias, cotangent,
    output, grad_out, summed, grad, bias_part,
):
    total = mine[...]
    for part in (first, second, third, fourth):
        total = total + part[...].astype(jnp.float32)
    high = total.astype(jnp.bfloat16)
    low = (total - high.astype(jnp.float32)).astype(jnp.bfloat16)
    kernel = weight[...]
    pre = jnp.dot(high, kernel, preferred_element_type=jnp.float32)
    pre = pre + jnp.dot(low, kernel, preferred_element_type=jnp.float32) + bias[...]
    gate = 1.0 / (1.0 + jnp.exp(-pre))
    output[...] = (pre * gate).astype(jnp.bfloat16)
    exact = cotangent[...].astype(jnp.float32) * (gate * (1.0 + pre * (1.0 - gate)))
    grad[...] = exact.astype(jnp.bfloat16)
    grad_out[...] = lax.dot_general(
        kernel, grad[...], (((1,), (1,)), ((), ())), preferred_element_type=jnp.float32
    ).astype(jnp.bfloat16)
    summed[...] = high
    bias_part[...] = jnp.sum(exact, axis=0, keepdims=True)


def split_tail(row):
    high = row.astype(jnp.bfloat16).astype(jnp.float32)
    lines = lax.broadcasted_iota(jnp.int32, (TAIL, row.shape[1]), 0)
    return jnp.where(lines == 0, high, jnp.where(lines == 1, row - high, 0.0))


def weight_kernel(summed, grad, bias_part, mine, near, across, far, product):
    column = lax.axis_index("col")
    product[...] = lax.dot_general(
        summed[...], grad[...], (((0,), (0,)), ((), ())), preferred_element_type=jnp.float32
    )
    tail = split_tail(bias_part[...])
    share = mine.shape[0] - TAIL
    for relative, out in enumerate((mine, near, across, far)):
        start = pl.multiple_of((column ^ relative) * share, share)
        rows = product[pl.ds(start, share), :]
        out[...] = jnp.concatenate([rows, tail], axis=0).astype(out.dtype)


def column_sum_kernel(mine, near, across, far, message):
    total = mine[...]
    for part in (near, across, far):
        total = total + part[...].astype(jnp.float32)
    share = total.shape[0] - TAIL
    tail = split_tail(total[share : share + 1] + total[share + 1 : share + 2])
    total = jnp.concatenate([total[:share], tail], axis=0).astype(jnp.bfloat16)
    message[...] = jnp.broadcast_to(total[None], message.shape)


def backward_kernel(
    count, target, source, values, local, first, second, third, fourth,
    mine, across, leaving, table, totals,
):
    column = lax.axis_index("col")
    live = count[0, 0]
    row = lax.axis_index("row")
    offsets = [0] + [offset_at(route, row)[1] for route in BACKWARD]
    for offset, part in zip(offsets, (local, first, second, third, fourth)):
        for block in range(VB):
            table[(HALF + offset) * VB + block] = part[:, block * BLK : (block + 1) * BLK]
    totals[...] = jnp.zeros_like(totals)

    def step(slot):
        goal = jnp.where(slot < live, source[0, 0, slot], totals.shape[0] - 1)
        totals[goal] += jnp.dot(
            table[target[0, 0, slot]], values[0, 0, slot], preferred_element_type=jnp.float32
        )

    for_slots(values.shape[2], live, step)
    outs = (mine, leaving.at[0], across, leaving.at[1])
    for relative, out in enumerate(outs):
        for block in range(VB):
            out[:, block * BLK : (block + 1) * BLK] = totals[
                (column ^ relative) * VB + block
            ].astype(out.dtype)


def source_pair_kernel(mine, across, arrived, kept, leaving):
    kept[...] = mine[...] + arrived[0].astype(jnp.float32)
    leaving[...] = (across[...] + arrived[1].astype(jnp.float32)).astype(leaving.dtype)


def row_sum_kernel(scale, received, after, part, bias_out):
    del after
    total = jnp.sum(received[...].astype(jnp.float32), axis=0) * scale
    share = part.shape[0]
    part[...] = total[:share].astype(part.dtype)
    bias_out[...] = total[share : share + 1] + total[share + 1 : share + 2]


def last_kernel(mine, arrived, output_in, bias_in, grad_inputs, output, bias_out):
    total = mine[...] + arrived[...].astype(jnp.float32)
    grad_inputs[...] = total.T.astype(jnp.bfloat16)
    output[...] = output_in[...]
    bias_out[...] = bias_in[...]


def join_kernel(own, near, across, far, grad_weight):
    column = lax.axis_index("col")
    share = own.shape[0]
    for relative, part in enumerate((own, near, across, far)):
        start = pl.multiple_of((column ^ relative) * share, share)
        grad_weight[pl.ds(start, share), :] = part[...].astype(jnp.float32)


def shards(
    features, weight, bias, block_values, block_target, block_source, block_count, cotangent
):
    columns = lax.axis_size("col")
    assert columns == 4
    rows = lax.axis_size("row")
    own_rows, width = features.shape
    slots = block_values.shape[2]
    sources = columns * VB
    bf16, f32 = jnp.bfloat16, jnp.float32

    values, own, bias = call(
        stage_kernel,
        [
            jax.ShapeDtypeStruct(block_values.shape, bf16),
            jax.ShapeDtypeStruct(features.shape, bf16),
            jax.ShapeDtypeStruct((1, width), f32),
        ],
        [pltpu.SemaphoreType.DMA] * 3,
        LONG,
        [pltpu.HBM] * 3,
        "stage",
    )(block_values, features, bias[None, :])
    near = swapped(features, "col", 1)
    across = swapped(features, "col", 2)
    far = swapped(across, "col", 1)
    head = call(
        table_kernel,
        [jax.ShapeDtypeStruct((sources - VB, BLK, width), bf16)],
        [],
        LONG,
        [VMEM] * 3,
        "feature_table",
    )(own, near, across)[0]
    whole = jax.ShapeDtypeStruct((own_rows, width), bf16)
    wide = jax.ShapeDtypeStruct((own_rows, width), f32)
    mine, *leaving = call(
        forward_kernel,
        [wide] + [whole] * 4,
        [
            pltpu.VMEM((sources, BLK, width), bf16),
            pltpu.VMEM((SPAN * VB + 1, BLK, width), f32),
        ],
        2 * slots * BLK * BLK * width,
        [SMEM] * 3 + [VMEM] * 3,
        "aggregate_terms",
    )(block_count, block_target, block_source, values, head, far)

    arrived = [routed(block, route) for block, route in zip(leaving, FORWARD)]
    flipped = jax.ShapeDtypeStruct((width, own_rows), bf16)
    output, grad_out, summed, grad, bias_part = call(
        middle_kernel,
        [whole, flipped, whole, whole, jax.ShapeDtypeStruct((1, width), f32)],
        [],
        2 * 3 * own_rows * width * width,
        [VMEM] * 8,
        "pointwise",
    )(mine, *arrived, weight, bias, cotangent)

    arrived = [routed(grad_out, route) for route in BACKWARD]
    share = width // columns
    packed = (share + TAIL, width)
    weight_mine, weight_near, weight_across, weight_far = call(
        weight_kernel,
        [jax.ShapeDtypeStruct(packed, f32)] + [jax.ShapeDtypeStruct(packed, bf16)] * 3,
        [pltpu.VMEM((width, width), f32)],
        LONG,
        [VMEM] * 3,
        "weight_term",
    )(summed, grad, bias_part)
    message = call(
        column_sum_kernel,
        [jax.ShapeDtypeStruct((rows,) + packed, bf16)],
        [],
        LONG,
        [VMEM] * 4,
        "weight_column_sum",
    )(
        weight_mine,
        swapped(weight_near, "col", 1),
        swapped(weight_across, "col", 2),
        swapped(weight_far, "col", 3),
    )[0]
    tall = jax.ShapeDtypeStruct((width, own_rows), f32)
    mine, across, leaving = call(
        backward_kernel,
        [tall, tall, jax.ShapeDtypeStruct((2, width, own_rows), bf16)],
        [
            pltpu.VMEM((SPAN * VB, width, BLK), bf16),
            pltpu.VMEM((sources + 1, width, BLK), f32),
        ],
        LONG,
        [SMEM] * 3 + [VMEM] * 6,
        "source_terms",
    )(
        block_count, block_target, block_source, values,
        grad_out, *arrived,
    )
    kept, leaving = call(
        source_pair_kernel, [tall, flipped], [], 0, [VMEM] * 3, "source_pair_sum"
    )(mine, across, swapped(leaving, "col", 1))
    across = swapped(leaving, "col", 2)

    scale = 1.0 / math.sqrt(own_rows * rows * columns)
    if rows > 8:
        received = lax.psum(message[:1].astype(f32), "row")
    else:
        received = lax.all_to_all(message, "row", 0, 0, tiled=True)
    part, bias_total = call(
        functools.partial(row_sum_kernel, scale),
        [jax.ShapeDtypeStruct((share, width), bf16), jax.ShapeDtypeStruct((1, width), f32)],
        [],
        LONG,
        [VMEM, pl.ANY],
        "weight_row_sum",
    )(received, mine)
    parts = [part] + [swapped(part, "col", bit) for bit in (1, 2, 3)]

    grad_inputs, output, bias_total = call(
        last_kernel,
        [whole, whole, jax.ShapeDtypeStruct((1, width), f32)],
        [],
        LONG,
        [VMEM] * 4,
        "source_sum",
    )(kept, across, output, bias_total)
    grad_weight = call(
        join_kernel, [jax.ShapeDtypeStruct((width, width), f32)], [], LONG, [VMEM] * 4, "weight_join"
    )(*parts)[0]
    return (output, grad_inputs, grad_weight, bias_total[0])


def solution(mesh):
    return jax.shard_map(
        shards,
        mesh=mesh,
        in_specs=(
            P(("row", "col"), None),
            P(),
            P(),
            P("row", "col", None, None, None),
            P("row", "col", None),
            P("row", "col", None),
            P("row", "col"),
            P(("row", "col"), None),
        ),
        out_specs=(P(("row", "col"), None), P(("row", "col"), None), P(), P()),
        check_vma=False,
    )
```

```python
import functools
import math

import jax
import jax.numpy as jnp
from jax import lax
from jax.experimental import pallas as pl
from jax.experimental.pallas import tpu as pltpu
from jax.sharding import PartitionSpec as P

BLK = 128
HALF = 2
VB = 2
SPAN = 2 * HALF + 1
TAIL = 8
FORWARD = ((1, None), (2, None), (-2, None), (-1, None))
BACKWARD = ((-1, None), (-2, None), (1, None), (2, None))
LONG = 10**11
VMEM = pltpu.VMEM
SMEM = pltpu.SMEM


def offset_at(route, row):
    reach, phase = route
    if phase is None:
        return reach, -reach
    toward = reach * (1 - 2 * lax.rem(row // reach + phase, 2))
    return toward, toward


def routed(block, route):
    size = lax.axis_size("row")
    reach, phase = route
    pairs = []
    for i in range(size):
        if phase is None:
            pairs.append((i, (i + reach) % size))
        else:
            pairs.append((i, (i + reach * (1 - 2 * ((i // reach + phase) % 2))) % size))
    return lax.ppermute(block, "row", pairs)


def swapped(block, axis, bit):
    size = lax.axis_size(axis)
    return lax.ppermute(block, axis, [(i, i ^ bit) for i in range(size)])


def spec(space):
    return pl.BlockSpec(memory_space=space)


def call(body, outs, scratch, flops, spaces, name):
    return pl.pallas_call(
        body,
        out_shape=outs,
        in_specs=[spec(space) for space in spaces],
        out_specs=[spec(VMEM)] * len(outs),
        scratch_shapes=scratch,
        name=name,
        cost_estimate=pl.CostEstimate(flops=flops, bytes_accessed=2**20, transcendentals=0),
        compiler_params=pltpu.CompilerParams(vmem_limit_bytes=16 * 2**20),
    )


def for_slots(slot_total, live, step):
    split = slot_total * 3 // 4
    for start, stop in ((0, split), (split, slot_total)):

        @pl.when(start < live)
        def _group():
            for slot in range(start, stop):
                step(slot)


def stage_kernel(values, own, bias, values_out, own_out, bias_out, values_sem, own_sem, bias_sem):
    copies = (
        pltpu.make_async_copy(values, values_out, values_sem),
        pltpu.make_async_copy(own, own_out, own_sem),
        pltpu.make_async_copy(bias, bias_out, bias_sem),
    )
    for copy in copies:
        copy.start()
    for copy in copies:
        copy.wait()


def table_kernel(own, near, across, head):
    for relative, part in enumerate((own, near, across)):
        for block in range(VB):
            head[relative * VB + block] = part[block * BLK : (block + 1) * BLK, :]


def forward_kernel(
    count, target, source, values, head, far,
    mine, first, second, third, fourth, table, totals,
):
    column = lax.axis_index("col")
    live = count[0, 0]
    known = head.shape[0]
    table[:known] = head[...]
    for block in range(VB):
        table[known + block] = far[block * BLK : (block + 1) * BLK, :]
    totals[...] = jnp.zeros_like(totals)

    def step(slot):
        block = source[0, 0, slot]
        place = ((block // VB) ^ column) * VB + lax.rem(block, VB)
        goal = jnp.where(slot < live, target[0, 0, slot], SPAN * VB)
        totals[goal] += jnp.dot(
            values[0, 0, slot], table[place], preferred_element_type=jnp.float32
        )

    for_slots(values.shape[2], live, step)
    row = lax.axis_index("row")
    offsets = [0] + [offset_at(route, row)[0] for route in FORWARD]
    for offset, out in zip(offsets, (mine, first, second, third, fourth)):
        for block in range(VB):
            out[block * BLK : (block + 1) * BLK, :] = totals[
                (HALF + offset) * VB + block
            ].astype(out.dtype)


def middle_kernel(
    mine, first, second, third, fourth, weight, bias, cotangent,
    output, grad_out, summed, grad, bias_part,
):
    total = mine[...]
    for part in (first, second, third, fourth):
        total = total + part[...].astype(jnp.float32)
    high = total.astype(jnp.bfloat16)
    low = (total - high.astype(jnp.float32)).astype(jnp.bfloat16)
    kernel = weight[...]
    pre = jnp.dot(high, kernel, preferred_element_type=jnp.float32)
    pre = pre + jnp.dot(low, kernel, preferred_element_type=jnp.float32) + bias[...]
    gate = 1.0 / (1.0 + jnp.exp(-pre))
    output[...] = (pre * gate).astype(jnp.bfloat16)
    exact = cotangent[...].astype(jnp.float32) * (gate * (1.0 + pre * (1.0 - gate)))
    grad[...] = exact.astype(jnp.bfloat16)
    grad_out[...] = lax.dot_general(
        kernel, grad[...], (((1,), (1,)), ((), ())), preferred_element_type=jnp.float32
    ).astype(jnp.bfloat16)
    summed[...] = high
    bias_part[...] = jnp.sum(exact, axis=0, keepdims=True)


def split_tail(row):
    high = row.astype(jnp.bfloat16).astype(jnp.float32)
    lines = lax.broadcasted_iota(jnp.int32, (TAIL, row.shape[1]), 0)
    return jnp.where(lines == 0, high, jnp.where(lines == 1, row - high, 0.0))


def weight_kernel(summed, grad, bias_part, mine, near, across, far, product):
    column = lax.axis_index("col")
    product[...] = lax.dot_general(
        summed[...], grad[...], (((0,), (0,)), ((), ())), preferred_element_type=jnp.float32
    )
    tail = split_tail(bias_part[...])
    share = mine.shape[0] - TAIL
    for relative, out in enumerate((mine, near, across, far)):
        start = pl.multiple_of((column ^ relative) * share, share)
        rows = product[pl.ds(start, share), :]
        out[...] = jnp.concatenate([rows, tail], axis=0).astype(out.dtype)


def column_sum_kernel(mine, near, across, far, message):
    total = mine[...]
    for part in (near, across, far):
        total = total + part[...].astype(jnp.float32)
    share = total.shape[0] - TAIL
    tail = split_tail(total[share : share + 1] + total[share + 1 : share + 2])
    total = jnp.concatenate([total[:share], tail], axis=0).astype(jnp.bfloat16)
    message[...] = jnp.broadcast_to(total[None], message.shape)


def backward_kernel(
    count, target, source, values, local, first, second, third, fourth,
    mine, across, leaving, table, totals,
):
    column = lax.axis_index("col")
    live = count[0, 0]
    row = lax.axis_index("row")
    offsets = [0] + [offset_at(route, row)[1] for route in BACKWARD]
    for offset, part in zip(offsets, (local, first, second, third, fourth)):
        for block in range(VB):
            table[(HALF + offset) * VB + block] = part[:, block * BLK : (block + 1) * BLK]
    totals[...] = jnp.zeros_like(totals)

    def step(slot):
        goal = jnp.where(slot < live, source[0, 0, slot], totals.shape[0] - 1)
        totals[goal] += jnp.dot(
            table[target[0, 0, slot]], values[0, 0, slot], preferred_element_type=jnp.float32
        )

    for_slots(values.shape[2], live, step)
    outs = (mine, leaving.at[0], across, leaving.at[1])
    for relative, out in enumerate(outs):
        for block in range(VB):
            out[:, block * BLK : (block + 1) * BLK] = totals[
                (column ^ relative) * VB + block
            ].astype(out.dtype)


def source_pair_kernel(mine, across, arrived, kept, leaving):
    kept[...] = mine[...] + arrived[0].astype(jnp.float32)
    leaving[...] = (across[...] + arrived[1].astype(jnp.float32)).astype(leaving.dtype)


def row_sum_kernel(scale, received, after, part, bias_out):
    del after
    total = jnp.sum(received[...].astype(jnp.float32), axis=0) * scale
    share = part.shape[0]
    part[...] = total[:share].astype(part.dtype)
    bias_out[...] = total[share : share + 1] + total[share + 1 : share + 2]


def last_kernel(mine, arrived, output_in, bias_in, grad_inputs, output, bias_out):
    total = mine[...] + arrived[...].astype(jnp.float32)
    grad_inputs[...] = total.T.astype(jnp.bfloat16)
    output[...] = output_in[...]
    bias_out[...] = bias_in[...]


def join_kernel(own, near, across, far, grad_weight):
    column = lax.axis_index("col")
    share = own.shape[0]
    for relative, part in enumerate((own, near, across, far)):
        start = pl.multiple_of((column ^ relative) * share, share)
        grad_weight[pl.ds(start, share), :] = part[...].astype(jnp.float32)


def shards(
    features, weight, bias, block_values, block_target, block_source, block_count, cotangent
):
    columns = lax.axis_size("col")
    assert columns == 4
    rows = lax.axis_size("row")
    own_rows, width = features.shape
    slots = block_values.shape[2]
    sources = columns * VB
    bf16, f32 = jnp.bfloat16, jnp.float32

    values, own, bias = call(
        stage_kernel,
        [
            jax.ShapeDtypeStruct(block_values.shape, bf16),
            jax.ShapeDtypeStruct(features.shape, bf16),
            jax.ShapeDtypeStruct((1, width), f32),
        ],
        [pltpu.SemaphoreType.DMA] * 3,
        LONG,
        [pltpu.HBM] * 3,
        "stage",
    )(block_values, features, bias[None, :])
    near = swapped(features, "col", 1)
    across = swapped(features, "col", 2)
    far = swapped(across, "col", 1)
    head = call(
        table_kernel,
        [jax.ShapeDtypeStruct((sources - VB, BLK, width), bf16)],
        [],
        LONG,
        [VMEM] * 3,
        "feature_table",
    )(own, near, across)[0]
    whole = jax.ShapeDtypeStruct((own_rows, width), bf16)
    wide = jax.ShapeDtypeStruct((own_rows, width), f32)
    mine, *leaving = call(
        forward_kernel,
        [wide] + [whole] * 4,
        [
            pltpu.VMEM((sources, BLK, width), bf16),
            pltpu.VMEM((SPAN * VB + 1, BLK, width), f32),
        ],
        2 * slots * BLK * BLK * width,
        [SMEM] * 3 + [VMEM] * 3,
        "aggregate_terms",
    )(block_count, block_target, block_source, values, head, far)

    arrived = [routed(block, route) for block, route in zip(leaving, FORWARD)]
    flipped = jax.ShapeDtypeStruct((width, own_rows), bf16)
    output, grad_out, summed, grad, bias_part = call(
        middle_kernel,
        [whole, flipped, whole, whole, jax.ShapeDtypeStruct((1, width), f32)],
        [],
        2 * 3 * own_rows * width * width,
        [VMEM] * 8,
        "pointwise",
    )(mine, *arrived, weight, bias, cotangent)

    arrived = [routed(grad_out, route) for route in BACKWARD]
    share = width // columns
    packed = (share + TAIL, width)
    weight_mine, weight_near, weight_across, weight_far = call(
        weight_kernel,
        [jax.ShapeDtypeStruct(packed, f32)] + [jax.ShapeDtypeStruct(packed, bf16)] * 3,
        [pltpu.VMEM((width, width), f32)],
        LONG,
        [VMEM] * 3,
        "weight_term",
    )(summed, grad, bias_part)
    message = call(
        column_sum_kernel,
        [jax.ShapeDtypeStruct((rows,) + packed, bf16)],
        [],
        LONG,
        [VMEM] * 4,
        "weight_column_sum",
    )(
        weight_mine,
        swapped(weight_near, "col", 1),
        swapped(weight_across, "col", 2),
        swapped(weight_far, "col", 3),
    )[0]
    tall = jax.ShapeDtypeStruct((width, own_rows), f32)
    mine, across, leaving = call(
        backward_kernel,
        [tall, tall, jax.ShapeDtypeStruct((2, width, own_rows), bf16)],
        [
            pltpu.VMEM((SPAN * VB, width, BLK), bf16),
            pltpu.VMEM((sources + 1, width, BLK), f32),
        ],
        LONG,
        [SMEM] * 3 + [VMEM] * 6,
        "source_terms",
    )(
        block_count, block_target, block_source, values,
        grad_out, *arrived,
    )
    kept, leaving = call(
        source_pair_kernel, [tall, flipped], [], 0, [VMEM] * 3, "source_pair_sum"
    )(mine, across, swapped(leaving, "col", 1))
    across = swapped(leaving, "col", 2)

    scale = 1.0 / math.sqrt(own_rows * rows * columns)
    if rows > 8:
        received = lax.psum(message[:1].astype(f32), "row")
    else:
        received = lax.all_to_all(message, "row", 0, 0, tiled=True)
    part, bias_total = call(
        functools.partial(row_sum_kernel, scale),
        [jax.ShapeDtypeStruct((share, width), bf16), jax.ShapeDtypeStruct((1, width), f32)],
        [],
        LONG,
        [VMEM, pl.ANY],
        "weight_row_sum",
    )(received, mine)
    parts = [part] + [swapped(part, "col", bit) for bit in (1, 2, 3)]

    grad_inputs, output, bias_total = call(
        last_kernel,
        [whole, whole, jax.ShapeDtypeStruct((1, width), f32)],
        [],
        LONG,
        [VMEM] * 4,
        "source_sum",
    )(kept, across, output, bias_total)
    grad_weight = call(
        join_kernel, [jax.ShapeDtypeStruct((width, width), f32)], [], LONG, [VMEM] * 4, "weight_join"
    )(*parts)[0]
    return (output, grad_inputs, grad_weight, bias_total[0])


def solution(mesh):
    return jax.shard_map(
        shards,
        mesh=mesh,
        in_specs=(
            P(("row", "col"), None),
            P(),
            P(),
            P("row", "col", None, None, None),
            P("row", "col", None),
            P("row", "col", None),
            P("row", "col"),
            P(("row", "col"), None),
        ),
        out_specs=(P(("row", "col"), None), P(("row", "col"), None), P(), P()),
        check_vma=False,
    )
```

```python
import functools
import math

import jax
import jax.numpy as jnp
from jax import lax
from jax.experimental import pallas as pl
from jax.experimental.pallas import tpu as pltpu
from jax.sharding import PartitionSpec as P

BLK = 128
HALF = 2
VB = 2
SPAN = 2 * HALF + 1
TAIL = 8
FORWARD = ((1, None), (2, None), (-2, None), (-1, None))
BACKWARD = ((-1, None), (-2, None), (1, None), (2, None))
LONG = 10**11
VMEM = pltpu.VMEM
SMEM = pltpu.SMEM


def offset_at(route, row):
    reach, phase = route
    if phase is None:
        return reach, -reach
    toward = reach * (1 - 2 * lax.rem(row // reach + phase, 2))
    return toward, toward


def routed(block, route):
    size = lax.axis_size("row")
    reach, phase = route
    pairs = []
    for i in range(size):
        if phase is None:
            pairs.append((i, (i + reach) % size))
        else:
            pairs.append((i, (i + reach * (1 - 2 * ((i // reach + phase) % 2))) % size))
    return lax.ppermute(block, "row", pairs)


def swapped(block, axis, bit):
    size = lax.axis_size(axis)
    return lax.ppermute(block, axis, [(i, i ^ bit) for i in range(size)])


def spec(space):
    return pl.BlockSpec(memory_space=space)


def call(body, outs, scratch, flops, spaces, name):
    return pl.pallas_call(
        body,
        out_shape=outs,
        in_specs=[spec(space) for space in spaces],
        out_specs=[spec(VMEM)] * len(outs),
        scratch_shapes=scratch,
        name=name,
        cost_estimate=pl.CostEstimate(flops=flops, bytes_accessed=2**20, transcendentals=0),
        compiler_params=pltpu.CompilerParams(vmem_limit_bytes=16 * 2**20),
    )


def for_slots(slot_total, split, live, step):
    for start, stop in ((0, split), (split, slot_total)):

        if start == stop:
            continue

        @pl.when(start < live)
        def _group():
            for slot in range(start, stop):
                step(slot)


def stage_kernel(values, own, bias, values_out, own_out, bias_out, values_sem, own_sem, bias_sem):
    copies = (
        pltpu.make_async_copy(values, values_out, values_sem),
        pltpu.make_async_copy(own, own_out, own_sem),
        pltpu.make_async_copy(bias, bias_out, bias_sem),
    )
    for copy in copies:
        copy.start()
    for copy in copies:
        copy.wait()


def table_kernel(own, near, across, head):
    for relative, part in enumerate((own, near, across)):
        for block in range(VB):
            head[relative * VB + block] = part[block * BLK : (block + 1) * BLK, :]


def forward_kernel(
    count, target, source, values, head, far,
    mine, first, second, third, fourth, table, totals,
):
    column = lax.axis_index("col")
    live = count[0, 0]
    known = head.shape[0]
    table[:known] = head[...]
    for block in range(VB):
        table[known + block] = far[block * BLK : (block + 1) * BLK, :]
    totals[...] = jnp.zeros_like(totals)

    def step(slot):
        block = source[0, 0, slot]
        place = ((block // VB) ^ column) * VB + lax.rem(block, VB)
        goal = jnp.where(slot < live, target[0, 0, slot], SPAN * VB)
        totals[goal] += jnp.dot(
            values[0, 0, slot], table[place], preferred_element_type=jnp.float32
        )

    for_slots(values.shape[2], values.shape[2] * 3 // 4, live, step)
    row = lax.axis_index("row")
    offsets = [0] + [offset_at(route, row)[0] for route in FORWARD]
    for offset, out in zip(offsets, (mine, first, second, third, fourth)):
        for block in range(VB):
            out[block * BLK : (block + 1) * BLK, :] = totals[
                (HALF + offset) * VB + block
            ].astype(out.dtype)


def middle_kernel(
    mine, first, second, third, fourth, weight, bias, cotangent,
    output, grad_out, summed, grad, bias_part,
):
    total = mine[...]
    for part in (first, second, third, fourth):
        total = total + part[...].astype(jnp.float32)
    high = total.astype(jnp.bfloat16)
    low = (total - high.astype(jnp.float32)).astype(jnp.bfloat16)
    kernel = weight[...]
    pre = jnp.dot(high, kernel, preferred_element_type=jnp.float32)
    pre = pre + jnp.dot(low, kernel, preferred_element_type=jnp.float32) + bias[...]
    gate = 1.0 / (1.0 + jnp.exp(-pre))
    output[...] = (pre * gate).astype(jnp.bfloat16)
    exact = cotangent[...].astype(jnp.float32) * (gate * (1.0 + pre * (1.0 - gate)))
    grad[...] = exact.astype(jnp.bfloat16)
    grad_out[...] = lax.dot_general(
        kernel, grad[...], (((1,), (1,)), ((), ())), preferred_element_type=jnp.float32
    ).astype(jnp.bfloat16)
    summed[...] = high
    bias_part[...] = jnp.sum(exact, axis=0, keepdims=True)


def split_tail(row):
    high = row.astype(jnp.bfloat16).astype(jnp.float32)
    lines = lax.broadcasted_iota(jnp.int32, (TAIL, row.shape[1]), 0)
    return jnp.where(lines == 0, high, jnp.where(lines == 1, row - high, 0.0))


def weight_kernel(summed, grad, bias_part, mine, near, across, far, product):
    column = lax.axis_index("col")
    product[...] = lax.dot_general(
        summed[...], grad[...], (((0,), (0,)), ((), ())), preferred_element_type=jnp.float32
    )
    tail = split_tail(bias_part[...])
    share = mine.shape[0] - TAIL
    for relative, out in enumerate((mine, near, across, far)):
        start = pl.multiple_of((column ^ relative) * share, share)
        rows = product[pl.ds(start, share), :]
        out[...] = jnp.concatenate([rows, tail], axis=0).astype(out.dtype)


def column_sum_kernel(mine, near, across, far, message):
    total = mine[...]
    for part in (near, across, far):
        total = total + part[...].astype(jnp.float32)
    share = total.shape[0] - TAIL
    tail = split_tail(total[share : share + 1] + total[share + 1 : share + 2])
    total = jnp.concatenate([total[:share], tail], axis=0).astype(jnp.bfloat16)
    message[...] = jnp.broadcast_to(total[None], message.shape)


def backward_kernel(
    count, target, source, values, local, first, second, third, fourth,
    mine, across, leaving, table, totals,
):
    column = lax.axis_index("col")
    live = count[0, 0]
    row = lax.axis_index("row")
    offsets = [0] + [offset_at(route, row)[1] for route in BACKWARD]
    for offset, part in zip(offsets, (local, first, second, third, fourth)):
        for block in range(VB):
            table[(HALF + offset) * VB + block] = part[:, block * BLK : (block + 1) * BLK]
    totals[...] = jnp.zeros_like(totals)

    def step(slot):
        goal = jnp.where(slot < live, source[0, 0, slot], totals.shape[0] - 1)
        totals[goal] += jnp.dot(
            table[target[0, 0, slot]], values[0, 0, slot], preferred_element_type=jnp.float32
        )

    for_slots(values.shape[2], values.shape[2], live, step)
    outs = (mine, leaving.at[0], across, leaving.at[1])
    for relative, out in enumerate(outs):
        for block in range(VB):
            out[:, block * BLK : (block + 1) * BLK] = totals[
                (column ^ relative) * VB + block
            ].astype(out.dtype)


def source_pair_kernel(mine, across, arrived, kept, leaving):
    kept[...] = mine[...] + arrived[0].astype(jnp.float32)
    leaving[...] = (across[...] + arrived[1].astype(jnp.float32)).astype(leaving.dtype)


def row_sum_kernel(scale, received, after, part, bias_out):
    del after
    total = jnp.sum(received[...].astype(jnp.float32), axis=0) * scale
    share = part.shape[0]
    part[...] = total[:share].astype(part.dtype)
    bias_out[...] = total[share : share + 1] + total[share + 1 : share + 2]


def last_kernel(mine, arrived, output_in, bias_in, grad_inputs, output, bias_out):
    total = mine[...] + arrived[...].astype(jnp.float32)
    grad_inputs[...] = total.T.astype(jnp.bfloat16)
    output[...] = output_in[...]
    bias_out[...] = bias_in[...]


def join_kernel(own, near, across, far, grad_weight):
    column = lax.axis_index("col")
    share = own.shape[0]
    for relative, part in enumerate((own, near, across, far)):
        start = pl.multiple_of((column ^ relative) * share, share)
        grad_weight[pl.ds(start, share), :] = part[...].astype(jnp.float32)


def shards(
    features, weight, bias, block_values, block_target, block_source, block_count, cotangent
):
    columns = lax.axis_size("col")
    assert columns == 4
    rows = lax.axis_size("row")
    own_rows, width = features.shape
    slots = block_values.shape[2]
    sources = columns * VB
    bf16, f32 = jnp.bfloat16, jnp.float32

    values, own, bias = call(
        stage_kernel,
        [
            jax.ShapeDtypeStruct(block_values.shape, bf16),
            jax.ShapeDtypeStruct(features.shape, bf16),
            jax.ShapeDtypeStruct((1, width), f32),
        ],
        [pltpu.SemaphoreType.DMA] * 3,
        LONG,
        [pltpu.HBM] * 3,
        "stage",
    )(block_values, features, bias[None, :])
    near = swapped(features, "col", 1)
    across = swapped(features, "col", 2)
    far = swapped(across, "col", 1)
    head = call(
        table_kernel,
        [jax.ShapeDtypeStruct((sources - VB, BLK, width), bf16)],
        [],
        LONG,
        [VMEM] * 3,
        "feature_table",
    )(own, near, across)[0]
    whole = jax.ShapeDtypeStruct((own_rows, width), bf16)
    wide = jax.ShapeDtypeStruct((own_rows, width), f32)
    mine, *leaving = call(
        forward_kernel,
        [wide] + [whole] * 4,
        [
            pltpu.VMEM((sources, BLK, width), bf16),
            pltpu.VMEM((SPAN * VB + 1, BLK, width), f32),
        ],
        2 * slots * BLK * BLK * width,
        [SMEM] * 3 + [VMEM] * 3,
        "aggregate_terms",
    )(block_count, block_target, block_source, values, head, far)

    arrived = [routed(block, route) for block, route in zip(leaving, FORWARD)]
    flipped = jax.ShapeDtypeStruct((width, own_rows), bf16)
    output, grad_out, summed, grad, bias_part = call(
        middle_kernel,
        [whole, flipped, whole, whole, jax.ShapeDtypeStruct((1, width), f32)],
        [],
        2 * 3 * own_rows * width * width,
        [VMEM] * 8,
        "pointwise",
    )(mine, *arrived, weight, bias, cotangent)

    arrived = [routed(grad_out, route) for route in BACKWARD]
    share = width // columns
    packed = (share + TAIL, width)
    weight_mine, weight_near, weight_across, weight_far = call(
        weight_kernel,
        [jax.ShapeDtypeStruct(packed, f32)] + [jax.ShapeDtypeStruct(packed, bf16)] * 3,
        [pltpu.VMEM((width, width), f32)],
        LONG,
        [VMEM] * 3,
        "weight_term",
    )(summed, grad, bias_part)
    message = call(
        column_sum_kernel,
        [jax.ShapeDtypeStruct((rows,) + packed, bf16)],
        [],
        LONG,
        [VMEM] * 4,
        "weight_column_sum",
    )(
        weight_mine,
        swapped(weight_near, "col", 1),
        swapped(weight_across, "col", 2),
        swapped(weight_far, "col", 3),
    )[0]
    tall = jax.ShapeDtypeStruct((width, own_rows), f32)
    mine, across, leaving = call(
        backward_kernel,
        [tall, tall, jax.ShapeDtypeStruct((2, width, own_rows), bf16)],
        [
            pltpu.VMEM((SPAN * VB, width, BLK), bf16),
            pltpu.VMEM((sources + 1, width, BLK), f32),
        ],
        LONG,
        [SMEM] * 3 + [VMEM] * 6,
        "source_terms",
    )(
        block_count, block_target, block_source, values,
        grad_out, *arrived,
    )
    kept, leaving = call(
        source_pair_kernel, [tall, flipped], [], 0, [VMEM] * 3, "source_pair_sum"
    )(mine, across, swapped(leaving, "col", 1))
    across = swapped(leaving, "col", 2)

    scale = 1.0 / math.sqrt(own_rows * rows * columns)
    if rows > 8:
        received = lax.psum(message[:1].astype(f32), "row")
    else:
        received = lax.all_to_all(message, "row", 0, 0, tiled=True)
    part, bias_total = call(
        functools.partial(row_sum_kernel, scale),
        [jax.ShapeDtypeStruct((share, width), bf16), jax.ShapeDtypeStruct((1, width), f32)],
        [],
        LONG,
        [VMEM, pl.ANY],
        "weight_row_sum",
    )(received, mine)
    parts = [part] + [swapped(part, "col", bit) for bit in (1, 2, 3)]

    grad_inputs, output, bias_total = call(
        last_kernel,
        [whole, whole, jax.ShapeDtypeStruct((1, width), f32)],
        [],
        LONG,
        [VMEM] * 4,
        "source_sum",
    )(kept, across, output, bias_total)
    grad_weight = call(
        join_kernel, [jax.ShapeDtypeStruct((width, width), f32)], [], LONG, [VMEM] * 4, "weight_join"
    )(*parts)[0]
    return (output, grad_inputs, grad_weight, bias_total[0])


def solution(mesh):
    return jax.shard_map(
        shards,
        mesh=mesh,
        in_specs=(
            P(("row", "col"), None),
            P(),
            P(),
            P("row", "col", None, None, None),
            P("row", "col", None),
            P("row", "col", None),
            P("row", "col"),
            P(("row", "col"), None),
        ),
        out_specs=(P(("row", "col"), None), P(("row", "col"), None), P(), P()),
        check_vma=False,
    )
```
